512 devices in a mesh: owner: 64 (over z, x, core), col: 8 (over y).
Axes of the slice: x: 4, y: 8, z: 8, core: 2. Of those that a mesh axis runs over, the one named last changes fastest.
Arguments:
- ks_tiles: bfloat16 [8192, 128, 128], P(('owner', 'col')), may hold values from -0.21875 to 0.21875
- chem_shift: float32 [1], replicated, may hold values from -0.4 to 0.4
- spectral_scale: float32 [1], replicated, may hold values from 1.25 to 2
- sub_tiles: int32 [512, 6, 6], replicated, may hold values from -1 to 8191, as said below
- result_dest: int32 [512, 6], replicated, may hold values from -1 to 8191, as said below
Outputs:
- density_tiles: float32 [8192, 128, 128], P(('owner', 'col'))
- electrons: float32 [1], replicated
The draws below stay inside these ranges and needn't reach their ends.
Inputs may be any that keep to these rules, and one draw needn't show every extreme that they name: `sub_tiles`: -1 marks a zero block. An entry t names a tile held by the device of mesh index t // 16 (owner index times the number of col devices plus col index); that owner index differs from the owner index of device s by at most one, cyclically. At most 2 entries of one submatrix name tiles of one device, and in every submatrix some device holds exactly 2 of its nonzero blocks. `result_dest`: -1 drops the block. An entry t names a tile of a device with the col index of device s and an owner index that differs from that of device s by at most one, cyclically. At most 3 entries of one submatrix go to one device, and every submatrix sends exactly 3 to some device. Blocks sent to the same tile are added.
All inputs are finite; a program needn't handle non-finite values.
Results may differ from the reference program's by a relative error of at most 0.0003.
Values may be sent and summed in bfloat16 or wider, within the bound.
A program may use at most 64 MiB of HBM per device.

```python
import math
import jax
import jax.numpy as jnp
from jax import lax

B = 128
S = 6
TPD = 16
ITERS = 2
SUBS = 512
TILES = 8192
N_OWNER = 64
N_COL = 8


def place_sources(first_key, second_key, hot_source, choices, room, positions):
    pool_list = jnp.repeat(jnp.arange(choices, dtype=jnp.int32), room)
    scores = jax.random.permutation(first_key, choices * room).astype(jnp.int32)
    scores = scores + choices * room * (pool_list == hot_source).astype(jnp.int32)
    sort_order = jnp.argsort(scores)
    remaining = pool_list[sort_order][:positions - room]
    chosen = jnp.concatenate([jnp.full((room,), hot_source, jnp.int32), remaining])
    marker = jnp.concatenate([jnp.ones((room,), jnp.int32), jnp.zeros((positions - room,), jnp.int32)])
    places = jax.random.permutation(second_key, positions)
    picked = jnp.zeros((positions,), jnp.int32).at[places].set(chosen)
    hot_place = jnp.zeros((positions,), jnp.int32).at[places].set(marker)
    return (picked, hot_place)


def draw_sub_tiles(key, part):
    key = jax.random.fold_in(key, 11)
    positions = S * S
    near_count = 3 * N_COL
    room = max(2, (positions + near_count - 1) // near_count)

    def draw_one(sub_key, sub_index):
        subkeys = jax.random.split(sub_key, 5)
        near_index = jnp.arange(near_count, dtype=jnp.int32)
        owner_here = sub_index // N_COL
        candidates = (owner_here + near_index // N_COL - 1 + N_OWNER) % N_OWNER * N_COL + near_index % N_COL
        hot_source = jax.random.randint(subkeys[0], (), 0, near_count)
        picked, hot_place = place_sources(subkeys[1], subkeys[2], hot_source, near_count, room, positions)
        store_slot = jax.random.randint(subkeys[3], (positions,), 0, TPD)
        tile_id = jnp.take(candidates, picked) * TPD + store_slot
        zeroed = (jax.random.randint(subkeys[4], (positions,), 0, 6) == 0) & (hot_place == 0)
        return jnp.where(zeroed, -1, tile_id).reshape(S, S).astype(jnp.int32)
    sub_count = N_OWNER * N_COL
    return jax.vmap(draw_one)(jax.random.split(key, sub_count), jnp.arange(sub_count, dtype=jnp.int32))


def draw_result_dest(key, part):
    key = jax.random.fold_in(key, 23)
    room = S // 2

    def draw_one(sub_key, sub_index):
        subkeys = jax.random.split(sub_key, 5)
        owner_here = sub_index // N_COL
        column_here = sub_index % N_COL
        hot_source = jax.random.randint(subkeys[0], (), 0, 3)
        picked, hot_place = place_sources(subkeys[1], subkeys[2], hot_source, 3, room, S)
        owner_to = (owner_here + picked - 1 + N_OWNER) % N_OWNER
        store_slot = jax.random.randint(subkeys[3], (S,), 0, TPD)
        tile_id = (owner_to * N_COL + column_here) * TPD + store_slot
        dropped = (jax.random.randint(subkeys[4], (S,), 0, 6) == 0) & (hot_place == 0)
        return jnp.where(dropped, -1, tile_id).astype(jnp.int32)
    sub_count = N_OWNER * N_COL
    return jax.vmap(draw_one)(jax.random.split(key, sub_count), jnp.arange(sub_count, dtype=jnp.int32))


def block_scale(own_key, extent, cuts, low, largest):
    factor_of = 1.0
    for position, blocks in cuts:
        draws = jax.random.uniform(jax.random.fold_in(jax.random.fold_in(own_key, 6), position), (blocks,), jnp.float32, low / len(cuts), largest / len(cuts))
        factor_of = factor_of * jnp.repeat(jnp.exp(draws), extent[position] // blocks).reshape((-1,) + (1,) * (len(extent) - 1 - position))
    return factor_of


def bell_draw(own_key, shape, spread, most, shards=(), kind=jnp.bfloat16):
    entries = jax.random.normal(own_key, shape, jnp.float32) * spread
    if len(shards) > 0:
        entries = block_scale(own_key, shape, shards, -0.22, 0.18) * entries
    return jnp.clip(entries, min=-most, max=most).astype(kind)


def setup_inputs(seed: int = 0) -> dict:
    arg_keys = jax.random.split(jax.random.key(seed), 6)
    return {
        "ks_tiles": bell_draw(arg_keys[0], (TILES, B, B), (S * B) ** -0.5, 0.21875, ((0, 512),)),
        "chem_shift": jnp.clip(jax.random.uniform(arg_keys[1], (1,), jnp.float32, -0.4, 0.4), -0.4, 0.4),
        "spectral_scale": jnp.clip(jnp.exp(jax.random.uniform(arg_keys[2], (1,), jnp.float32, math.log(1.25), math.log(2.0))), 1.25, 2.0),
        "sub_tiles": draw_sub_tiles(jax.random.fold_in(arg_keys[5], 71), 0),
        "result_dest": draw_result_dest(jax.random.fold_in(arg_keys[5], 71), 0),
    }


def sign_density(tile_block, chem_shift, spectral_scale):
    blocks = tile_block.shape[0]
    edge_len = tile_block.shape[2]
    matrix_order = blocks * edge_len
    assembled = jnp.transpose(tile_block, (0, 2, 1, 3)).reshape(matrix_order, matrix_order)
    identity = jnp.eye(matrix_order, dtype=assembled.dtype)
    current = (0.5 * (assembled + assembled.T) - chem_shift[0] * identity) / spectral_scale[0]
    for sweep in range(ITERS):
        square = jnp.dot(current, current, precision=lax.Precision.HIGHEST, preferred_element_type=jnp.float32)
        cube_term = jnp.dot(current, square, precision=lax.Precision.HIGHEST, preferred_element_type=jnp.float32)
        current = 1.5 * current - 0.5 * cube_term
    return 0.5 * (identity - current)


def reference(ks_tiles, chem_shift, spectral_scale, sub_tiles, result_dest):
    def one_sub(tile_lists):
        flat_list = tile_lists.reshape(-1)
        picked = jnp.take(ks_tiles, jnp.maximum(flat_list, 0), axis=0).astype(jnp.float32)
        keep_mask = (flat_list >= 0).astype(jnp.float32)
        tile_block = (picked * keep_mask[:, None, None]).reshape(S, S, B, B)
        density = sign_density(tile_block, chem_shift, spectral_scale)
        return density[:, :B].reshape(S, B, B), jnp.trace(density[:B, :B])

    columns, traces = lax.map(one_sub, sub_tiles)
    flattened = columns.reshape(SUBS * S, B, B)
    target = result_dest.reshape(-1)
    target = jnp.where(target >= 0, target, TILES).astype(jnp.int32)
    density_tiles = jax.ops.segment_sum(flattened, target, num_segments=TILES + 1)[:TILES]
    electrons = (2.0 * jnp.sum(traces)).reshape(1)
    return density_tiles, electrons
```

```python
import functools
import jax
import jax.numpy as jnp
from jax import lax
from jax.experimental import pallas as pl
from jax.experimental.pallas import tpu as pltpu
from jax.sharding import PartitionSpec as P

F32 = jnp.float32
BF16 = jnp.bfloat16
MESH = pl.DeviceIdType.MESH
ROOM = 2
BACK = 3
FAR = 1 << 20


def log2(n):
    assert n & (n - 1) == 0
    return n.bit_length() - 1


def dot(a, b, contract):
    return lax.dot_general(a, b, (contract, ((), ())), preferred_element_type=F32)


def kernel(
    owners, columns, inner, blocks, chem_ref, scale_ref, tiles_ref, sub_ref, dest_ref,
    out_ref, elec_ref, lists, dests, packet, arrived, place, matrix, results, going, back,
    trace_out, trace_in, list_sem, send_sem, recv_sem, back_send, back_recv, trace_send, trace_recv,
):
    tiles_per, edge = tiles_ref.shape[0], tiles_ref.shape[1]
    outer = owners // inner
    owner = lax.axis_index("owner")
    column = lax.axis_index("col")
    myself = owner * columns + column
    tile_bits, column_bits = log2(tiles_per), log2(columns)
    near = [lax.rem(owner + owners + r - 1, owners) for r in range(3)]
    ring = [lax.rem(column + dy, columns) for dy in range(columns)]
    in_block = lax.rem(owner, inner)
    block_start = owner - in_block
    mates = [block_start + lax.rem(in_block + k, inner) for k in range(inner)]
    across = [lax.rem(owner + k * inner, owners) for k in range(outer)]

    barrier = pltpu.get_barrier_semaphore()
    partners = [(near[r], ring[dy]) for dy in range(columns) for r in range(3) if (r, dy) != (1, 0)]
    partners += [(mates[k], column) for k in range(1, inner)]
    partners += [(across[k], column) for k in range(1, outer)]
    for partner in partners:
        pl.semaphore_signal(barrier, inc=1, device_id=partner, device_id_type=MESH)

    fetches = []
    for r in range(3):
        rows = pl.ds(pl.multiple_of(near[r] * columns, columns), columns)
        fetches.append(pltpu.make_async_copy(sub_ref.at[rows], lists.at[r], list_sem.at[r]))
        fetches.append(pltpu.make_async_copy(dest_ref.at[rows], dests.at[r], list_sem.at[3 + r]))
    for fetch in fetches:
        fetch.start()
    for fetch in fetches:
        fetch.wait()

    shape = (blocks, blocks)
    spot = lax.broadcasted_iota(jnp.int32, shape, 0) * blocks + lax.broadcasted_iota(jnp.int32, shape, 1)
    hops = [0] + [s for d in range(1, columns // 2 + 1) for s in dict.fromkeys((d, columns - d))]
    for dy in hops:
        for r in range(3):
            asked = lists[r, ring[dy]]
            mine = lax.shift_right_arithmetic(asked, tile_bits) == myself
            code = spot * tiles_per + (asked & (tiles_per - 1))
            first = jnp.min(jnp.where(mine, code, FAR)) & (tiles_per - 1)
            last = jnp.max(jnp.where(mine, code, -1)) & (tiles_per - 1)
            if (r, dy) == (1, 0):
                slot = (columns + column) * ROOM
                arrived[slot] = tiles_ref[first]
                arrived[slot + 1] = tiles_ref[last]
            else:
                packet[r * columns + dy, 0] = tiles_ref[first]
                packet[r * columns + dy, 1] = tiles_ref[last]

    pl.semaphore_wait(barrier, len(partners))
    sends = []
    for dy in hops:
        for r in range(3):
            if (r, dy) == (1, 0):
                continue
            sends.append(
                pltpu.make_async_remote_copy(
                    src_ref=packet.at[r * columns + dy],
                    dst_ref=arrived.at[pl.ds(((2 - r) * columns + column) * ROOM, ROOM)],
                    send_sem=send_sem.at[r * columns + dy],
                    recv_sem=recv_sem.at[r * columns + dy],
                    device_id=(near[r], ring[dy]),
                    device_id_type=MESH,
                )
            )
            sends[-1].start()

    nothing = 3 * columns * ROOM
    arrived[nothing] = jnp.zeros((edge, edge), BF16)
    own = lists[1, column]
    source = lax.shift_right_arithmetic(own, tile_bits)
    offset = lax.shift_right_arithmetic(source, column_bits) - owner + (owners + 1)
    offset = jnp.where(offset >= owners, offset - owners, offset)
    offset = jnp.where(offset >= owners, offset - owners, offset)
    base = (offset * columns + (source & (columns - 1))) * ROOM
    for p in range(blocks * blocks):
        here = spot == p
        entry = jnp.sum(jnp.where(here, own, 0))
        start = jnp.sum(jnp.where(here, base, 0))
        same = source == lax.shift_right_arithmetic(entry, tile_bits)
        rank = (jnp.min(jnp.where(same, spot, FAR)) < p).astype(jnp.int32)
        place[p] = jnp.where(entry >= 0, jnp.clip(start + rank, 0, nothing), nothing)

    row = lax.broadcasted_iota(jnp.int32, (columns, blocks), 0)
    lane = lax.broadcasted_iota(jnp.int32, (columns, blocks), 1)
    targets = [
        [jnp.sum(jnp.where((row == column) & (lane == i), dests[r], 0)) for i in range(blocks)]
        for r in range(3)
    ]
    chosen = [[jnp.int32(blocks) for _ in range(BACK)] for _ in range(3)]
    stored = [[jnp.int32(-1) for _ in range(BACK)] for _ in range(3)]
    for r in range(3):
        taken = jnp.int32(0)
        sent = jnp.int32(0)
        for i in range(blocks):
            target = targets[r][i]
            home = lax.shift_right_arithmetic(target, tile_bits + column_bits)
            mine = (target >= 0) & (home == owner)
            for k in range(BACK):
                stored[r][k] = jnp.where(mine & (taken == k), target & (tiles_per - 1), stored[r][k])
            taken = taken + mine.astype(jnp.int32)
            target = targets[1][i]
            home = lax.shift_right_arithmetic(target, tile_bits + column_bits)
            theirs = (target >= 0) & (home == near[r])
            for k in range(BACK):
                chosen[r][k] = jnp.where(theirs & (sent == k), i, chosen[r][k])
            sent = sent + theirs.astype(jnp.int32)

    for send in sends:
        send.wait()

    for i in range(blocks):
        for j in range(blocks):
            matrix[pl.ds(i * edge, edge), pl.ds(j * edge, edge)] = arrived[place[i * blocks + j]]

    chem = chem_ref[0]
    inverse = 1.0 / scale_ref[0]
    order = blocks * edge
    wide = 2 * edge

    def apply(u):
        high = u.astype(BF16)
        low = (u - high.astype(F32)).astype(BF16)
        both = jnp.concatenate([high, low], axis=0)
        parts = []
        for start in range(0, order, wide):
            cut = pl.ds(start, wide)
            w = dot(both, matrix[:, cut], ((1,), (0,))) + dot(both, matrix[cut, :], ((1,), (1,)))
            parts.append(0.5 * (w[:edge] + w[edge:]) - chem * u[:, start : start + wide])
        return jnp.concatenate(parts, axis=1) * inverse

    diagonal = lax.broadcasted_iota(jnp.int32, (edge, edge), 0) == lax.broadcasted_iota(
        jnp.int32, (edge, edge), 1
    )
    parts = []
    for j in range(blocks):
        upper = matrix[pl.ds(0, edge), pl.ds(j * edge, edge)].astype(F32)
        lower = matrix[pl.ds(j * edge, edge), pl.ds(0, edge)].astype(F32)
        part = 0.5 * (upper + lower.T)
        if j == 0:
            part = part - jnp.where(diagonal, chem, 0.0)
        parts.append(part * inverse)
    start = jnp.concatenate(parts, axis=1)
    first = 1.5 * start - 0.5 * apply(apply(start))
    once = apply(first)
    square = 1.5 * once - 0.5 * apply(apply(once))
    trace = 1.5 * jnp.sum(jnp.where(diagonal, first[:, :edge], 0.0)) - 0.5 * jnp.sum(first * square)
    trace = 0.5 * (edge - trace)

    groups = (
        (columns, column, [(owner, ring[k]) for k in range(columns)]),
        (inner, in_block, [(mates[k], column) for k in range(inner)]),
        (outer, lax.div(owner, inner), [(across[k], column) for k in range(outer)]),
    )

    def give(stage, value):
        count, at, group = groups[stage]
        trace_out[stage] = value
        trace_in[stage, at] = value
        copies = []
        for k in range(1, count):
            copies.append(
                pltpu.make_async_remote_copy(
                    src_ref=trace_out.at[stage],
                    dst_ref=trace_in.at[stage, at],
                    send_sem=trace_send.at[stage, k],
                    recv_sem=trace_recv.at[stage, k],
                    device_id=group[k],
                    device_id_type=MESH,
                )
            )
            copies[-1].start()
        return copies

    def take(stage, copies):
        for copy in copies:
            copy.wait()
        total = trace_in[stage, 0]
        for k in range(1, groups[stage][0]):
            total = total + trace_in[stage, k]
        return total

    copies = give(0, jnp.full((8, 128), trace, F32))
    once = apply(square)
    cube = 1.5 * once - 0.5 * apply(apply(once))
    last = 1.5 * first - 0.5 * cube
    for i in range(blocks):
        part = last[:, i * edge : (i + 1) * edge].T
        results[i] = 0.5 * (jnp.where(diagonal, 1.0, 0.0) - part) if i == 0 else -0.5 * part
    results[blocks] = jnp.zeros((edge, edge), F32)
    returns = []
    for r in (0, 2, 1):
        for k in range(BACK):
            if r == 1:
                back[1, k] = results[chosen[r][k]]
            else:
                going[r // 2, k] = results[chosen[r][k]]
        if r != 1:
            returns.append(
                pltpu.make_async_remote_copy(
                    src_ref=going.at[r // 2],
                    dst_ref=back.at[2 - r],
                    send_sem=back_send.at[r // 2],
                    recv_sem=back_recv.at[r // 2],
                    device_id=(near[r], column),
                    device_id_type=MESH,
                )
            )
            returns[-1].start()
    copies = give(1, take(0, copies))
    copies = give(2, take(1, copies))
    for copy in returns:
        copy.wait()
    weights = [
        [jnp.where(stored[r][k] == t, 1.0, 0.0).astype(F32) for r in range(3) for k in range(BACK)]
        for t in range(tiles_per)
    ]
    for at in range(0, edge, 8):
        pieces = [back[r, k, pl.ds(at, 8)] for r in range(3) for k in range(BACK)]
        for t in range(tiles_per):
            total = weights[t][0] * pieces[0]
            for weight, piece in zip(weights[t][1:], pieces[1:]):
                total = total + weight * piece
            out_ref[t, pl.ds(at, 8)] = total
    elec_ref[0] = 2.0 * jnp.max(take(2, copies))


def on_device(ks_tiles, chem_shift, spectral_scale, sub_tiles, result_dest):
    owners = lax.axis_size("owner")
    columns = lax.axis_size("col")
    tiles_per, edge = ks_tiles.shape[0], ks_tiles.shape[1]
    blocks = sub_tiles.shape[1]
    order = blocks * edge
    inner = min(8, owners)
    outer = owners // inner
    widest = max(columns, inner, outer)
    vmem, smem, hbm = pltpu.VMEM, pltpu.SMEM, pl.ANY
    dma = pltpu.SemaphoreType.DMA
    return pl.pallas_call(
        functools.partial(kernel, owners, columns, inner, blocks),
        out_shape=(
            jax.ShapeDtypeStruct((tiles_per, edge, edge), F32),
            jax.ShapeDtypeStruct((1,), F32),
        ),
        in_specs=[pl.BlockSpec(memory_space=s) for s in (smem, smem, vmem, hbm, hbm)],
        out_specs=[pl.BlockSpec(memory_space=s) for s in (vmem, smem)],
        scratch_shapes=[
            vmem((3, columns, blocks, blocks), jnp.int32),
            vmem((3, columns, blocks), jnp.int32),
            vmem((3 * columns, ROOM, edge, edge), BF16),
            vmem((3 * columns * ROOM + 1, edge, edge), BF16),
            smem((blocks * blocks,), jnp.int32),
            vmem((order, order), BF16),
            vmem((blocks + 1, edge, edge), F32),
            vmem((2, BACK, edge, edge), F32),
            vmem((3, BACK, edge, edge), F32),
            vmem((3, 8, 128), F32),
            vmem((3, widest, 8, 128), F32),
            dma((6,)),
            dma((3 * columns,)),
            dma((3 * columns,)),
            dma((2,)),
            dma((2,)),
            dma((3, widest)),
            dma((3, widest)),
        ],
        compiler_params=pltpu.CompilerParams(
            collective_id=0, has_side_effects=True, vmem_limit_bytes=48 * 2**20
        ),
        name="submatrix_density",
    )(chem_shift, spectral_scale, ks_tiles, sub_tiles, result_dest)


def solution(mesh):
    return jax.shard_map(
        on_device,
        mesh=mesh,
        in_specs=(P(("owner", "col"), None, None), P(), P(), P(), P()),
        out_specs=(P(("owner", "col"), None, None), P()),
        check_vma=False,
    )
```

```python
import functools
import jax
import jax.numpy as jnp
from jax import lax
from jax.experimental import pallas as pl
from jax.experimental.pallas import tpu as pltpu
from jax.sharding import PartitionSpec as P

F32 = jnp.float32
BF16 = jnp.bfloat16
MESH = pl.DeviceIdType.MESH
ROOM = 2
BACK = 3
FAR = 1 << 20


def log2(n):
    assert n & (n - 1) == 0
    return n.bit_length() - 1


def dot(a, b):
    return jnp.dot(a, b, preferred_element_type=F32)


def kernel(
    owners, columns, inner, blocks, chem_ref, scale_ref, tiles_hbm, sub_hbm, dest_hbm,
    out_ref, elec_ref, tiles_ref, lists, dests, packet, passing, arrived, place, high, low,
    results, going, back, trace_out, trace_in, fetch_sem, pass_sem, send_sem, recv_sem, back_send, back_recv,
    trace_send, trace_recv,
):
    tiles_per, edge = tiles_ref.shape[0], tiles_ref.shape[1]
    devices = owners * columns
    outer = owners // inner
    owner = lax.axis_index("owner")
    column = lax.axis_index("col")
    myself = owner * columns + column
    tile_bits, column_bits = log2(tiles_per), log2(columns)
    near = [lax.rem(owner + owners + r - 1, owners) for r in range(3)]
    ring = [lax.rem(column + dy, columns) for dy in range(columns)]
    in_block = lax.rem(owner, inner)
    block_start = owner - in_block
    mates = [block_start + lax.rem(in_block + k, inner) for k in range(inner)]
    across = [lax.rem(owner + k * inner, owners) for k in range(outer)]

    fetches = [
        pltpu.make_async_copy(there, here, fetch_sem.at[n])
        for n, (there, here) in enumerate(
            (
                (sub_hbm, lists),
                (tiles_hbm, tiles_ref),
                (dest_hbm, dests),
            )
        )
    ]
    for fetch in fetches:
        fetch.start()
    barrier = pltpu.get_barrier_semaphore()
    partners = [(near[r], ring[dy]) for dy in range(columns) for r in range(3) if (r, dy) != (1, 0)]
    partners += [(mates[k], column) for k in range(1, inner)]
    partners += [(across[k], column) for k in range(1, outer)]
    for partner in partners:
        pl.semaphore_signal(barrier, inc=1, device_id=partner, device_id_type=MESH)
    pl.semaphore_wait(barrier, len(partners))

    half = columns // 2
    turn = 1 - 2 * (owner & 1)
    at = [lax.rem(column + turn * k + columns, columns) for k in range(columns)]
    before = at[columns - 1]
    step = pltpu.make_async_remote_copy(
        src_ref=tiles_hbm,
        dst_ref=passing,
        send_sem=pass_sem.at[0],
        recv_sem=pass_sem.at[1],
        device_id=(owner, at[1]),
        device_id_type=MESH,
    )
    step.start()
    for fetch in fetches:
        fetch.wait()

    shape = (blocks, devices)
    lane = lax.broadcasted_iota(jnp.int32, shape, 1)
    row = lax.broadcasted_iota(jnp.int32, shape, 0)

    def asked_of(source):
        least, most = jnp.full(shape, FAR, jnp.int32), jnp.full(shape, -1, jnp.int32)
        for i in range(blocks):
            asked = lists[i]
            mine = lax.shift_right_arithmetic(asked, tile_bits) == source
            code = (row + i * blocks) * tiles_per + (asked & (tiles_per - 1))
            least = jnp.minimum(least, jnp.where(mine, code, FAR))
            most = jnp.maximum(most, jnp.where(mine, code, -1))
        least = jnp.min(least, axis=0, keepdims=True) & (tiles_per - 1)
        most = jnp.max(most, axis=0, keepdims=True) & (tiles_per - 1)
        return least * tiles_per + most

    sends = []

    def pack(asked, tiles, r, to, ref, slot):
        both = jnp.sum(jnp.where(lane[:1] == near[r] * columns + to, asked, 0))
        ref[slot] = tiles[lax.shift_right_arithmetic(both, tile_bits)]
        ref[slot + 1] = tiles[both & (tiles_per - 1)]

    def send(asked, tiles, r, k, source, to):
        slot = (r * columns + k) * ROOM
        pack(asked, tiles, r, to, packet, slot)
        sends.append(
            pltpu.make_async_remote_copy(
                src_ref=packet.at[pl.ds(slot, ROOM)],
                dst_ref=arrived.at[pl.ds(((2 - r) * columns + source) * ROOM, ROOM)],
                send_sem=send_sem.at[r * columns + k],
                recv_sem=recv_sem.at[r * columns + k],
                device_id=(near[r], to),
                device_id_type=MESH,
            )
        )
        sends[-1].start()

    asked = asked_of(myself)
    for k in [*range(columns - 1, half, -1), 0]:
        for r in range(3):
            if (r, k) != (1, 0):
                send(asked, tiles_ref, r, k, column, at[k])
    pack(asked, tiles_ref, 1, column, arrived, (columns + column) * ROOM)
    asked = asked_of(owner * columns + before)

    nothing = 3 * columns * ROOM
    arrived[nothing] = jnp.zeros((edge, edge), BF16)
    across_i = lax.broadcasted_iota(jnp.int32, (blocks, blocks), 1)
    spot = across_i * blocks + lax.broadcasted_iota(jnp.int32, (blocks, blocks), 0)
    own = jnp.zeros((blocks, blocks), jnp.int32)
    for i in range(blocks):
        held = jnp.sum(jnp.where(lane == myself, lists[i], 0), axis=1, keepdims=True)
        own = own + jnp.where(across_i == i, held, 0)
    source = lax.shift_right_arithmetic(own, tile_bits)
    offset = lax.shift_right_arithmetic(source, column_bits) - owner + (owners + 1)
    offset = jnp.where(offset >= owners, offset - owners, offset)
    offset = jnp.where(offset >= owners, offset - owners, offset)
    base = (offset * columns + (source & (columns - 1))) * ROOM
    for p in range(blocks * blocks):
        here = spot == p
        entry = jnp.sum(jnp.where(here, own, 0))
        start = jnp.sum(jnp.where(here, base, 0))
        same = source == lax.shift_right_arithmetic(entry, tile_bits)
        rank = (jnp.min(jnp.where(same, spot, FAR)) < p).astype(jnp.int32)
        place[p] = jnp.where(entry >= 0, jnp.clip(start + rank, 0, nothing), nothing)

    step.wait()
    for k in range(half, 0, -1):
        for r in range(3):
            if (r, k) != (1, 1):
                send(asked, passing, r, k, before, at[k - 1])
    pack(asked, passing, 1, column, arrived, (columns + before) * ROOM)

    targets = [
        [
            jnp.sum(jnp.where((lane == near[r] * columns + column) & (row == i), dests[...], 0))
            for i in range(blocks)
        ]
        for r in range(3)
    ]
    chosen = [[jnp.int32(blocks) for _ in range(BACK)] for _ in range(3)]
    stored = [[jnp.int32(-1) for _ in range(BACK)] for _ in range(3)]
    for r in range(3):
        taken = jnp.int32(0)
        sent = jnp.int32(0)
        for i in range(blocks):
            target = targets[r][i]
            home = lax.shift_right_arithmetic(target, tile_bits + column_bits)
            mine = (target >= 0) & (home == owner)
            for k in range(BACK):
                stored[r][k] = jnp.where(mine & (taken == k), target & (tiles_per - 1), stored[r][k])
            taken = taken + mine.astype(jnp.int32)
            target = targets[1][i]
            home = lax.shift_right_arithmetic(target, tile_bits + column_bits)
            theirs = (target >= 0) & (home == near[r])
            for k in range(BACK):
                chosen[r][k] = jnp.where(theirs & (sent == k), i, chosen[r][k])
            sent = sent + theirs.astype(jnp.int32)

    for copy in sends:
        copy.wait()

    chem = chem_ref[...]
    inverse = 1.0 / scale_ref[...]
    order = blocks * edge
    wide = 2 * edge
    diagonal = lax.broadcasted_iota(jnp.int32, (edge, edge), 0) == lax.broadcasted_iota(
        jnp.int32, (edge, edge), 1
    )
    parts = []
    for i in range(blocks):
        for j in range(blocks):
            part = arrived[place[i * blocks + j]].astype(F32)
            part = part + arrived[place[j * blocks + i]].T.astype(F32)
            part = part * (0.5 * inverse)
            if i == j:
                part = part - jnp.where(diagonal, chem * inverse, 0.0)
            rows, cols = pl.ds(i * edge, edge), pl.ds(j * edge, edge)
            upper = part.astype(BF16)
            high[rows, cols] = upper
            low[rows, cols] = (part - upper.astype(F32)).astype(BF16)
            if i == 0:
                parts.append(part)
    start = jnp.concatenate(parts, axis=1)

    def apply(u):
        upper = u.astype(BF16)
        lower = (u - upper.astype(F32)).astype(BF16)
        both = jnp.concatenate([upper, lower], axis=0)
        parts = []
        for at in range(0, order, wide):
            cut = pl.ds(at, wide)
            w = dot(both, high[:, cut])
            parts.append(w[:edge] + w[edge:] + dot(upper, low[:, cut]))
        return jnp.concatenate(parts, axis=1)

    first = 1.5 * start - 0.5 * apply(apply(start))
    once = apply(first)
    twice = apply(once)
    cubed = 1.5 * jnp.sum(first * once) - 0.5 * jnp.sum(once * twice)
    trace = 1.5 * jnp.sum(jnp.where(diagonal, first[:, :edge], 0.0)) - 0.5 * cubed
    trace = 0.5 * (edge - trace)

    groups = (
        (columns, column, [(owner, ring[k]) for k in range(columns)]),
        (inner, in_block, [(mates[k], column) for k in range(inner)]),
        (outer, lax.div(owner, inner), [(across[k], column) for k in range(outer)]),
    )

    def give(stage, value):
        count, at, group = groups[stage]
        trace_out[stage] = value
        trace_in[stage, at] = value
        copies = []
        for k in range(1, count):
            copies.append(
                pltpu.make_async_remote_copy(
                    src_ref=trace_out.at[stage],
                    dst_ref=trace_in.at[stage, at],
                    send_sem=trace_send.at[stage, k],
                    recv_sem=trace_recv.at[stage, k],
                    device_id=group[k],
                    device_id_type=MESH,
                )
            )
            copies[-1].start()
        return copies

    def take(stage, copies):
        for copy in copies:
            copy.wait()
        total = trace_in[stage, 0]
        for k in range(1, groups[stage][0]):
            total = total + trace_in[stage, k]
        return total

    copies = give(0, jnp.full((8, 128), trace, F32))
    square = 1.5 * once - 0.5 * apply(twice)
    once = apply(square)
    copies = give(1, take(0, copies))
    twice = apply(once)
    cube = 1.5 * once - 0.5 * apply(twice)
    last = 1.5 * first - 0.5 * cube
    copies = give(2, take(1, copies))
    for i in range(blocks):
        part = last[:, i * edge : (i + 1) * edge].T
        results[i] = 0.5 * (jnp.where(diagonal, 1.0, 0.0) - part) if i == 0 else -0.5 * part
    results[blocks] = jnp.zeros((edge, edge), F32)
    returns = []
    for r in (0, 2, 1):
        for k in range(BACK):
            if r == 1:
                back[1, k] = results[chosen[r][k]]
            else:
                going[r // 2, k] = results[chosen[r][k]]
        if r != 1:
            returns.append(
                pltpu.make_async_remote_copy(
                    src_ref=going.at[r // 2],
                    dst_ref=back.at[2 - r],
                    send_sem=back_send.at[r // 2],
                    recv_sem=back_recv.at[r // 2],
                    device_id=(near[r], column),
                    device_id_type=MESH,
                )
            )
            returns[-1].start()
    for copy in returns:
        copy.wait()
    weights = [
        [jnp.where(stored[r][k] == t, 1.0, 0.0).astype(F32) for r in range(3) for k in range(BACK)]
        for t in range(tiles_per)
    ]
    for at in range(0, edge, 8):
        pieces = [back[r, k, pl.ds(at, 8)] for r in range(3) for k in range(BACK)]
        for t in range(tiles_per):
            total = weights[t][0] * pieces[0]
            for weight, piece in zip(weights[t][1:], pieces[1:]):
                total = total + weight * piece
            out_ref[t, pl.ds(at, 8)] = total
    elec_ref[...] = 2.0 * take(2, copies)[:1]


def on_device(ks_tiles, chem_shift, spectral_scale, sub_tiles, result_dest):
    owners = lax.axis_size("owner")
    columns = lax.axis_size("col")
    tiles_per, edge = ks_tiles.shape[0], ks_tiles.shape[1]
    blocks = sub_tiles.shape[1]
    order = blocks * edge
    inner = min(8, owners)
    outer = owners // inner
    widest = max(columns, inner, outer)
    vmem, smem, hbm = pltpu.VMEM, pltpu.SMEM, pl.ANY
    dma = pltpu.SemaphoreType.DMA
    density, electrons = pl.pallas_call(
        functools.partial(kernel, owners, columns, inner, blocks),
        out_shape=(
            jax.ShapeDtypeStruct((tiles_per, edge, edge), F32),
            jax.ShapeDtypeStruct((1, 128), F32),
        ),
        in_specs=[pl.BlockSpec(memory_space=vmem)] * 2 + [pl.BlockSpec(memory_space=hbm)] * 3,
        out_specs=[pl.BlockSpec(memory_space=vmem)] * 2,
        scratch_shapes=[
            vmem((tiles_per, edge, edge), BF16),
            vmem((blocks, blocks, owners * columns), jnp.int32),
            vmem((blocks, owners * columns), jnp.int32),
            vmem((3 * columns * ROOM, edge, edge), BF16),
            vmem((tiles_per, edge, edge), BF16),
            vmem((3 * columns * ROOM + 1, edge, edge), BF16),
            smem((blocks * blocks,), jnp.int32),
            vmem((order, order), BF16),
            vmem((order, order), BF16),
            vmem((blocks + 1, edge, edge), F32),
            vmem((2, BACK, edge, edge), F32),
            vmem((3, BACK, edge, edge), F32),
            vmem((3, 8, 128), F32),
            vmem((3, widest, 8, 128), F32),
            dma((3,)),
            dma((2,)),
            dma((3 * columns,)),
            dma((3 * columns,)),
            dma((2,)),
            dma((2,)),
            dma((3, widest)),
            dma((3, widest)),
        ],
        compiler_params=pltpu.CompilerParams(
            collective_id=0, has_side_effects=True, vmem_limit_bytes=48 * 2**20
        ),
        name="submatrix_density",
    )(
        chem_shift.reshape(1, 1),
        spectral_scale.reshape(1, 1),
        *(
            pltpu.with_memory_space_constraint(a, pltpu.HBM)
            for a in (
                ks_tiles,
                jnp.transpose(sub_tiles, (1, 2, 0)),
                result_dest.T,
            )
        )
    )
    return density, electrons[0, :1]


def solution(mesh):
    return jax.shard_map(
        on_device,
        mesh=mesh,
        in_specs=(P(("owner", "col"), None, None), P(), P(), P(), P()),
        out_specs=(P(("owner", "col"), None, None), P()),
        check_vma=False,
    )
```

```python
import functools
import itertools
import jax
import jax.numpy as jnp
from jax import lax
from jax.experimental import pallas as pl
from jax.experimental.pallas import tpu as pltpu
from jax.sharding import PartitionSpec as P

F32 = jnp.float32
BF16 = jnp.bfloat16
MESH = pl.DeviceIdType.MESH
ROOM = 2
BACK = 3
FAR = 1 << 20


def log2(n):
    assert n & (n - 1) == 0
    return n.bit_length() - 1


def dot(a, b):
    return jnp.dot(a, b, preferred_element_type=F32)


def kernel(
    owners, columns, blocks, chem_ref, scale_ref, tiles_hbm, sub_hbm, dest_hbm,
    out_ref, elec_ref, tiles_ref, lists, dests, packet, passing, arrived, place, high, low,
    results, going, back, trace_out, trace_in, fetch_sem, pass_sem, send_sem, recv_sem, back_send, back_recv,
    trace_send, trace_recv, ready,
):
    tiles_per, edge = tiles_ref.shape[0], tiles_ref.shape[1]
    devices = owners * columns
    owner = lax.axis_index("owner")
    column = lax.axis_index("col")
    myself = owner * columns + column
    tile_bits, column_bits = log2(tiles_per), log2(columns)
    near = [lax.rem(owner + owners + r - 1, owners) for r in range(3)]
    half = columns // 2
    core = owner & 1
    turn = 1 - 2 * core
    at = [lax.rem(column + turn * k + columns, columns) for k in range(columns)]
    before = at[columns - 1]

    fetches = [
        pltpu.make_async_copy(there, here, fetch_sem.at[n])
        for n, (there, here) in enumerate(
            (
                (sub_hbm, lists),
                (tiles_hbm, tiles_ref),
                (dest_hbm, dests),
            )
        )
    ]
    for fetch in fetches:
        fetch.start()
    beside = [(owner, at[1]), (owner, before), (near[0], column), (near[2], column)]
    barrier = pltpu.get_barrier_semaphore()

    def tell(sem, partners):
        for partner in partners:
            pl.semaphore_signal(sem, inc=1, device_id=partner, device_id_type=MESH)

    tell(barrier, beside)
    pl.semaphore_wait(barrier, len(beside))

    step = pltpu.make_async_remote_copy(
        src_ref=tiles_hbm,
        dst_ref=passing,
        send_sem=pass_sem.at[0],
        recv_sem=pass_sem.at[1],
        device_id=(owner, at[1]),
        device_id_type=MESH,
    )
    step.start()
    tell(ready.at[0], beside)
    for fetch in fetches:
        fetch.wait()

    shape = (blocks, devices)
    lane = lax.broadcasted_iota(jnp.int32, shape, 1)
    row = lax.broadcasted_iota(jnp.int32, shape, 0)

    def asked_of(source):
        least, most = jnp.full(shape, FAR, jnp.int32), jnp.full(shape, -1, jnp.int32)
        for i in range(blocks):
            asked = lists[i]
            mine = lax.shift_right_arithmetic(asked, tile_bits) == source
            code = (row + i * blocks) * tiles_per + (asked & (tiles_per - 1))
            least = jnp.minimum(least, jnp.where(mine, code, FAR))
            most = jnp.maximum(most, jnp.where(mine, code, -1))
        least = jnp.min(least, axis=0, keepdims=True) & (tiles_per - 1)
        most = jnp.max(most, axis=0, keepdims=True) & (tiles_per - 1)
        return least * tiles_per + most

    sends = []

    def pack(asked, tiles, r, to, ref, slot):
        both = jnp.sum(jnp.where(lane[:1] == near[r] * columns + to, asked, 0))
        ref[slot] = tiles[lax.shift_right_arithmetic(both, tile_bits)]
        ref[slot + 1] = tiles[both & (tiles_per - 1)]

    def send(asked, tiles, r, k, source, to):
        slot = (r * columns + k) * ROOM
        pack(asked, tiles, r, to, packet, slot)
        sends.append(
            pltpu.make_async_remote_copy(
                src_ref=packet.at[pl.ds(slot, ROOM)],
                dst_ref=arrived.at[pl.ds(((2 - r) * columns + source) * ROOM, ROOM)],
                send_sem=send_sem.at[r * columns + k],
                recv_sem=recv_sem.at[r * columns + k],
                device_id=(near[r], to),
                device_id_type=MESH,
            )
        )
        sends[-1].start()

    asked = asked_of(myself)
    pl.semaphore_wait(ready.at[0], len(beside))
    over = [(owner, at[2]), (owner, at[columns - 2])]
    tell(ready.at[1], over)
    for k in (columns - 1, 0):
        for r in range(3):
            if (r, k) != (1, 0):
                send(asked, tiles_ref, r, k, column, at[k])
    pl.semaphore_wait(ready.at[1], len(over))
    for k in range(columns - 2, half, -1):
        for r in range(3):
            send(asked, tiles_ref, r, k, column, at[k])
    pack(asked, tiles_ref, 1, column, arrived, (columns + column) * ROOM)
    asked = asked_of(owner * columns + before)

    nothing = 3 * columns * ROOM
    arrived[nothing] = jnp.zeros((edge, edge), BF16)
    across_i = lax.broadcasted_iota(jnp.int32, (blocks, blocks), 1)
    spot = across_i * blocks + lax.broadcasted_iota(jnp.int32, (blocks, blocks), 0)
    own = jnp.zeros((blocks, blocks), jnp.int32)
    for i in range(blocks):
        held = jnp.sum(jnp.where(lane == myself, lists[i], 0), axis=1, keepdims=True)
        own = own + jnp.where(across_i == i, held, 0)
    source = lax.shift_right_arithmetic(own, tile_bits)
    offset = lax.shift_right_arithmetic(source, column_bits) - owner + (owners + 1)
    offset = jnp.where(offset >= owners, offset - owners, offset)
    offset = jnp.where(offset >= owners, offset - owners, offset)
    base = (offset * columns + (source & (columns - 1))) * ROOM
    for p in range(blocks * blocks):
        here = spot == p
        entry = jnp.sum(jnp.where(here, own, 0))
        start = jnp.sum(jnp.where(here, base, 0))
        same = source == lax.shift_right_arithmetic(entry, tile_bits)
        rank = (jnp.min(jnp.where(same, spot, FAR)) < p).astype(jnp.int32)
        place[p] = jnp.where(entry >= 0, jnp.clip(start + rank, 0, nothing), nothing)

    step.wait()
    for k in range(half, 0, -1):
        for r in range(3):
            if (r, k) != (1, 1):
                send(asked, passing, r, k, before, at[k - 1])
    pack(asked, passing, 1, column, arrived, (columns + before) * ROOM)

    reach, stage = 1, 2
    while 2 * reach <= max(2, owners // 2):
        far = [
            (lax.rem(owner + reach, owners), column),
            (lax.rem(owner + owners - reach, owners), column),
        ]
        tell(ready.at[stage], far)
        pl.semaphore_wait(ready.at[stage], 2)
        reach, stage = 2 * reach, stage + 1

    targets = [
        [
            jnp.sum(jnp.where((lane == near[r] * columns + column) & (row == i), dests[...], 0))
            for i in range(blocks)
        ]
        for r in range(3)
    ]
    chosen = [[jnp.int32(blocks) for _ in range(BACK)] for _ in range(3)]
    stored = [[jnp.int32(-1) for _ in range(BACK)] for _ in range(3)]
    for r in range(3):
        taken = jnp.int32(0)
        sent = jnp.int32(0)
        for i in range(blocks):
            target = targets[r][i]
            home = lax.shift_right_arithmetic(target, tile_bits + column_bits)
            mine = (target >= 0) & (home == owner)
            for k in range(BACK):
                stored[r][k] = jnp.where(mine & (taken == k), target & (tiles_per - 1), stored[r][k])
            taken = taken + mine.astype(jnp.int32)
            target = targets[1][i]
            home = lax.shift_right_arithmetic(target, tile_bits + column_bits)
            theirs = (target >= 0) & (home == near[r])
            for k in range(BACK):
                chosen[r][k] = jnp.where(theirs & (sent == k), i, chosen[r][k])
            sent = sent + theirs.astype(jnp.int32)

    for copy in sends:
        copy.wait()

    chem = chem_ref[...]
    inverse = 1.0 / scale_ref[...]
    order = blocks * edge
    wide = 2 * edge
    diagonal = lax.broadcasted_iota(jnp.int32, (edge, edge), 0) == lax.broadcasted_iota(
        jnp.int32, (edge, edge), 1
    )
    parts = []
    for i, j in sorted(itertools.product(range(blocks), repeat=2), key=lambda p: (p[0] > 0, p[1])):
        part = arrived[place[i * blocks + j]].astype(F32)
        part = part + arrived[place[j * blocks + i]].T.astype(F32)
        part = part * (0.5 * inverse)
        if i == j:
            part = part - jnp.where(diagonal, chem * inverse, 0.0)
        rows, cols = pl.ds(i * edge, edge), pl.ds(j * edge, edge)
        upper = part.astype(BF16)
        high[rows, cols] = upper
        low[rows, cols] = (part - upper.astype(F32)).astype(BF16)
        if i == 0:
            parts.append(part)
    start = jnp.concatenate(parts, axis=1)

    def apply(u):
        upper = u.astype(BF16)
        lower = (u - upper.astype(F32)).astype(BF16)
        both = jnp.concatenate([upper, lower], axis=0)
        parts = []
        for at in range(0, order, wide):
            cut = pl.ds(at, wide)
            w = dot(both, high[:, cut])
            parts.append(w[:edge] + w[edge:] + dot(upper, low[:, cut]))
        return jnp.concatenate(parts, axis=1)

    first = 1.5 * start - 0.5 * apply(apply(start))
    once = apply(first)
    twice = apply(once)
    cubed = 1.5 * jnp.sum(first * once) - 0.5 * jnp.sum(once * twice)
    trace = 1.5 * jnp.sum(jnp.where(diagonal, first[:, :edge], 0.0)) - 0.5 * cubed
    trace = 0.5 * (edge - trace)

    inner = min(8, owners)
    width, depth = inner // 2, owners // inner
    here_x, here_z = lax.div(lax.rem(owner, inner), 2), lax.div(owner, inner)

    def steps(*sizes):
        every = list(itertools.product(*(range(size) for size in sizes)))[1:]
        return sorted(every, key=lambda p: -sum(min(n, size - n) for n, size in zip(p, sizes)))

    groups = (
        (
            2 * columns,
            core * columns + column,
            [
                (owner - core + lax.rem(core + dc, 2), lax.rem(column + dy, columns))
                for dy, dc in steps(columns, 2)
            ],
        ),
        (
            owners // 2,
            lax.div(owner, 2),
            [
                (
                    lax.rem(here_z + dz, depth) * inner + lax.rem(here_x + dx, width) * 2 + core,
                    column,
                )
                for dz, dx in steps(depth, width)
            ],
        ),
    )

    def give(stage, value):
        place_in = groups[stage][1]
        trace_out[stage] = value
        trace_in[stage, place_in] = value
        copies = []
        for k, partner in enumerate(groups[stage][2]):
            copies.append(
                pltpu.make_async_remote_copy(
                    src_ref=trace_out.at[stage],
                    dst_ref=trace_in.at[stage, place_in],
                    send_sem=trace_send.at[stage, k],
                    recv_sem=trace_recv.at[stage, k],
                    device_id=partner,
                    device_id_type=MESH,
                )
            )
            copies[-1].start()
        return copies

    def take(stage, copies):
        for copy in copies:
            copy.wait_recv()
        total = trace_in[stage, 0]
        for k in range(1, groups[stage][0]):
            total = total + trace_in[stage, k]
        return total

    first_copies = give(0, jnp.full((1, 128), trace, F32))
    square = 1.5 * once - 0.5 * apply(twice)
    once = apply(square)
    cube = 1.5 * once - 0.5 * apply(apply(once))
    last = 1.5 * first - 0.5 * cube
    for i in range(blocks):
        part = last[:, i * edge : (i + 1) * edge].T
        results[i] = 0.5 * (jnp.where(diagonal, 1.0, 0.0) - part) if i == 0 else -0.5 * part
    results[blocks] = jnp.zeros((edge, edge), F32)
    returns = []
    for r in (0, 2, 1):
        for k in range(BACK):
            if r == 1:
                back[1, k] = results[chosen[r][k]]
            else:
                going[r // 2, k] = results[chosen[r][k]]
        if r != 1:
            returns.append(
                pltpu.make_async_remote_copy(
                    src_ref=going.at[r // 2],
                    dst_ref=back.at[2 - r],
                    send_sem=back_send.at[r // 2],
                    recv_sem=back_recv.at[r // 2],
                    device_id=(near[r], column),
                    device_id_type=MESH,
                )
            )
            returns[-1].start()
    last_copies = give(1, take(0, first_copies))
    for copy in returns:
        copy.wait()
    weights = [
        [jnp.where(stored[r][k] == t, 1.0, 0.0).astype(F32) for r in range(3) for k in range(BACK)]
        for t in range(tiles_per)
    ]
    for at in range(0, edge, 8):
        pieces = [back[r, k, pl.ds(at, 8)] for r in range(3) for k in range(BACK)]
        for t in range(tiles_per):
            total = weights[t][0] * pieces[0]
            for weight, piece in zip(weights[t][1:], pieces[1:]):
                total = total + weight * piece
            out_ref[t, pl.ds(at, 8)] = total
    elec_ref[...] = 2.0 * take(1, last_copies)
    for copy in first_copies + last_copies:
        copy.wait_send()


def on_device(ks_tiles, chem_shift, spectral_scale, sub_tiles, result_dest):
    owners = lax.axis_size("owner")
    columns = lax.axis_size("col")
    tiles_per, edge = ks_tiles.shape[0], ks_tiles.shape[1]
    blocks = sub_tiles.shape[1]
    order = blocks * edge
    widest = max(2 * columns, owners // 2)
    vmem, smem, hbm = pltpu.VMEM, pltpu.SMEM, pl.ANY
    dma = pltpu.SemaphoreType.DMA
    density, electrons = pl.pallas_call(
        functools.partial(kernel, owners, columns, blocks),
        out_shape=(
            jax.ShapeDtypeStruct((tiles_per, edge, edge), F32),
            jax.ShapeDtypeStruct((1, 128), F32),
        ),
        in_specs=[pl.BlockSpec(memory_space=vmem)] * 2 + [pl.BlockSpec(memory_space=hbm)] * 3,
        out_specs=[pl.BlockSpec(memory_space=vmem)] * 2,
        scratch_shapes=[
            vmem((tiles_per, edge, edge), BF16),
            vmem((blocks, blocks, owners * columns), jnp.int32),
            vmem((blocks, owners * columns), jnp.int32),
            vmem((3 * columns * ROOM, edge, edge), BF16),
            vmem((tiles_per, edge, edge), BF16),
            vmem((3 * columns * ROOM + 1, edge, edge), BF16),
            smem((blocks * blocks,), jnp.int32),
            vmem((order, order), BF16),
            vmem((order, order), BF16),
            vmem((blocks + 1, edge, edge), F32),
            vmem((2, BACK, edge, edge), F32),
            vmem((3, BACK, edge, edge), F32),
            vmem((2, 1, 128), F32),
            vmem((2, widest, 1, 128), F32),
            dma((3,)),
            dma((2,)),
            dma((3 * columns,)),
            dma((3 * columns,)),
            dma((2,)),
            dma((2,)),
            dma((2, widest)),
            dma((2, widest)),
            pltpu.SemaphoreType.REGULAR((2 + log2(owners),)),
        ],
        compiler_params=pltpu.CompilerParams(
            collective_id=0, has_side_effects=True, vmem_limit_bytes=48 * 2**20
        ),
        name="submatrix_density",
    )(
        chem_shift.reshape(1, 1),
        spectral_scale.reshape(1, 1),
        *(
            pltpu.with_memory_space_constraint(a, pltpu.HBM)
            for a in (
                ks_tiles,
                jnp.transpose(sub_tiles, (1, 2, 0)),
                result_dest.T,
            )
        )
    )
    return density, electrons[0, :1]


def solution(mesh):
    return jax.shard_map(
        on_device,
        mesh=mesh,
        in_specs=(P(("owner", "col"), None, None), P(), P(), P(), P()),
        out_specs=(P(("owner", "col"), None, None), P()),
        check_vma=False,
    )
```

```python
import functools
import itertools
import jax
import jax.numpy as jnp
from jax import lax
from jax.experimental import pallas as pl
from jax.experimental.pallas import tpu as pltpu
from jax.sharding import PartitionSpec as P

F32 = jnp.float32
BF16 = jnp.bfloat16
MESH = pl.DeviceIdType.MESH
ROOM = 2
BACK = 3
FAR = 1 << 20


def log2(n):
    assert n & (n - 1) == 0
    return n.bit_length() - 1


def dot(a, b):
    return jnp.dot(a, b, preferred_element_type=F32)


def kernel(
    owners, columns, blocks, chem_ref, scale_ref, tiles_hbm, sub_hbm, dest_hbm,
    out_ref, elec_ref, tiles_ref, lists, dests, packet, passing, arrived, place, high, low,
    results, going, back, trace_out, trace_in, fetch_sem, pass_sem, send_sem, recv_sem, back_send, back_recv,
    trace_send, trace_recv, ready,
):
    tiles_per, edge = tiles_ref.shape[0], tiles_ref.shape[1]
    devices = owners * columns
    owner = lax.axis_index("owner")
    column = lax.axis_index("col")
    myself = owner * columns + column
    tile_bits, column_bits = log2(tiles_per), log2(columns)
    near = [lax.rem(owner + owners + r - 1, owners) for r in range(3)]
    half = columns // 2
    core = owner & 1
    turn = 1 - 2 * core
    at = [lax.rem(column + turn * k + columns, columns) for k in range(columns)]
    before = at[columns - 1]

    fetches = [
        pltpu.make_async_copy(there, here, fetch_sem.at[n])
        for n, (there, here) in enumerate(
            (
                (sub_hbm, lists),
                (tiles_hbm, tiles_ref),
                (dest_hbm, dests),
            )
        )
    ]
    for fetch in fetches:
        fetch.start()
    beside = [(owner, at[1]), (owner, before), (near[0], column), (near[2], column)]
    barrier = pltpu.get_barrier_semaphore()

    def tell(sem, partners):
        for partner in partners:
            pl.semaphore_signal(sem, inc=1, device_id=partner, device_id_type=MESH)

    tell(barrier, beside)
    pl.semaphore_wait(barrier, len(beside))

    step = pltpu.make_async_remote_copy(
        src_ref=tiles_hbm,
        dst_ref=passing,
        send_sem=pass_sem.at[0],
        recv_sem=pass_sem.at[1],
        device_id=(owner, at[1]),
        device_id_type=MESH,
    )
    step.start()
    tell(ready.at[0], beside)
    for fetch in fetches:
        fetch.wait()

    shape = (blocks, devices)
    lane = lax.broadcasted_iota(jnp.int32, shape, 1)
    row = lax.broadcasted_iota(jnp.int32, shape, 0)

    def asked_of(source):
        least, most = jnp.full(shape, FAR, jnp.int32), jnp.full(shape, -1, jnp.int32)
        for i in range(blocks):
            asked = lists[i]
            mine = lax.shift_right_arithmetic(asked, tile_bits) == source
            code = (row + i * blocks) * tiles_per + (asked & (tiles_per - 1))
            least = jnp.minimum(least, jnp.where(mine, code, FAR))
            most = jnp.maximum(most, jnp.where(mine, code, -1))
        least = jnp.min(least, axis=0, keepdims=True) & (tiles_per - 1)
        most = jnp.max(most, axis=0, keepdims=True) & (tiles_per - 1)
        return least * tiles_per + most

    sends = []

    def pack(asked, tiles, r, to, ref, slot):
        both = jnp.sum(jnp.where(lane[:1] == near[r] * columns + to, asked, 0))
        ref[slot] = tiles[lax.shift_right_arithmetic(both, tile_bits)]
        ref[slot + 1] = tiles[both & (tiles_per - 1)]

    def send(asked, tiles, r, k, source, to):
        slot = (r * columns + k) * ROOM
        pack(asked, tiles, r, to, packet, slot)
        sends.append(
            pltpu.make_async_remote_copy(
                src_ref=packet.at[pl.ds(slot, ROOM)],
                dst_ref=arrived.at[pl.ds(((2 - r) * columns + source) * ROOM, ROOM)],
                send_sem=send_sem.at[r * columns + k],
                recv_sem=recv_sem.at[r * columns + k],
                device_id=(near[r], to),
                device_id_type=MESH,
            )
        )
        sends[-1].start()

    asked = asked_of(myself)
    pl.semaphore_wait(ready.at[0], len(beside))
    over = [(owner, at[2]), (owner, at[columns - 2])]
    tell(ready.at[1], over)
    for k in (columns - 1, 0):
        for r in range(3):
            if (r, k) != (1, 0):
                send(asked, tiles_ref, r, k, column, at[k])
    pl.semaphore_wait(ready.at[1], len(over))
    for k in range(columns - 2, half, -1):
        for r in range(3):
            send(asked, tiles_ref, r, k, column, at[k])
    pack(asked, tiles_ref, 1, column, arrived, (columns + column) * ROOM)
    asked = asked_of(owner * columns + before)

    nothing = 3 * columns * ROOM
    arrived[nothing] = jnp.zeros((edge, edge), BF16)
    across_i = lax.broadcasted_iota(jnp.int32, (blocks, blocks), 1)
    spot = across_i * blocks + lax.broadcasted_iota(jnp.int32, (blocks, blocks), 0)
    own = jnp.zeros((blocks, blocks), jnp.int32)
    for i in range(blocks):
        held = jnp.sum(jnp.where(lane == myself, lists[i], 0), axis=1, keepdims=True)
        own = own + jnp.where(across_i == i, held, 0)
    source = lax.shift_right_arithmetic(own, tile_bits)
    offset = lax.shift_right_arithmetic(source, column_bits) - owner + (owners + 1)
    offset = jnp.where(offset >= owners, offset - owners, offset)
    offset = jnp.where(offset >= owners, offset - owners, offset)
    base = (offset * columns + (source & (columns - 1))) * ROOM
    for p in range(blocks * blocks):
        here = spot == p
        entry = jnp.sum(jnp.where(here, own, 0))
        start = jnp.sum(jnp.where(here, base, 0))
        same = source == lax.shift_right_arithmetic(entry, tile_bits)
        rank = (jnp.min(jnp.where(same, spot, FAR)) < p).astype(jnp.int32)
        place[p] = jnp.where(entry >= 0, jnp.clip(start + rank, 0, nothing), nothing)

    step.wait()
    for k in range(half, 0, -1):
        for r in range(3):
            if (r, k) != (1, 1):
                send(asked, passing, r, k, before, at[k - 1])
    pack(asked, passing, 1, column, arrived, (columns + before) * ROOM)

    reach, stage = 1, 2
    while 2 * reach <= max(2, owners // 2):
        far = [
            (lax.rem(owner + reach, owners), column),
            (lax.rem(owner + owners - reach, owners), column),
        ]
        tell(ready.at[stage], far)
        pl.semaphore_wait(ready.at[stage], 2)
        reach, stage = 2 * reach, stage + 1

    targets = [
        [
            jnp.sum(jnp.where((lane == near[r] * columns + column) & (row == i), dests[...], 0))
            for i in range(blocks)
        ]
        for r in range(3)
    ]
    chosen = [[jnp.int32(blocks) for _ in range(BACK)] for _ in range(3)]
    stored = [[jnp.int32(-1) for _ in range(BACK)] for _ in range(3)]
    for r in range(3):
        taken = jnp.int32(0)
        sent = jnp.int32(0)
        for i in range(blocks):
            target = targets[r][i]
            home = lax.shift_right_arithmetic(target, tile_bits + column_bits)
            mine = (target >= 0) & (home == owner)
            for k in range(BACK):
                stored[r][k] = jnp.where(mine & (taken == k), target & (tiles_per - 1), stored[r][k])
            taken = taken + mine.astype(jnp.int32)
            target = targets[1][i]
            home = lax.shift_right_arithmetic(target, tile_bits + column_bits)
            theirs = (target >= 0) & (home == near[r])
            for k in range(BACK):
                chosen[r][k] = jnp.where(theirs & (sent == k), i, chosen[r][k])
            sent = sent + theirs.astype(jnp.int32)

    for copy in sends:
        copy.wait()

    chem = chem_ref[...]
    inverse = 1.0 / scale_ref[...]
    order = blocks * edge
    wide = 2 * edge
    diagonal = lax.broadcasted_iota(jnp.int32, (edge, edge), 0) == lax.broadcasted_iota(
        jnp.int32, (edge, edge), 1
    )
    parts = []
    for i, j in sorted(itertools.product(range(blocks), repeat=2), key=lambda p: (p[0] > 0, p[1])):
        part = arrived[place[i * blocks + j]].astype(F32)
        part = part + arrived[place[j * blocks + i]].T.astype(F32)
        part = part * (0.5 * inverse)
        if i == j:
            part = part - jnp.where(diagonal, chem * inverse, 0.0)
        rows, cols = pl.ds(i * edge, edge), pl.ds(j * edge, edge)
        upper = part.astype(BF16)
        high[rows, cols] = upper
        low[rows, cols] = (part - upper.astype(F32)).astype(BF16)
        if i == 0:
            parts.append(part)
    start = jnp.concatenate(parts, axis=1)

    def apply(u):
        upper = u.astype(BF16)
        lower = (u - upper.astype(F32)).astype(BF16)
        both = jnp.concatenate([upper, lower], axis=0)
        parts = []
        for at in range(0, order, wide):
            cut = pl.ds(at, wide)
            w = dot(both, high[:, cut])
            parts.append(w[:edge] + w[edge:] + dot(upper, low[:, cut]))
        return jnp.concatenate(parts, axis=1)

    first = 1.5 * start - 0.5 * apply(apply(start))
    once = apply(first)
    twice = apply(once)
    cubed = 1.5 * jnp.sum(first * once) - 0.5 * jnp.sum(once * twice)
    trace = 1.5 * jnp.sum(jnp.where(diagonal, first[:, :edge], 0.0)) - 0.5 * cubed
    trace = 0.5 * (edge - trace)

    inner = min(8, owners)
    width, depth = inner // 2, owners // inner
    here_x, here_z = lax.div(lax.rem(owner, inner), 2), lax.div(owner, inner)

    def steps(*sizes):
        every = list(itertools.product(*(range(size) for size in sizes)))[1:]
        return sorted(every, key=lambda p: -sum(min(n, size - n) for n, size in zip(p, sizes)))

    groups = (
        (columns, column, [(owner, lax.rem(column + dy, columns)) for (dy,) in steps(columns)]),
        (
            owners,
            owner,
            [
                (
                    lax.rem(here_z + dz, depth) * inner
                    + lax.rem(here_x + dx, width) * 2
                    + lax.rem(core + dc, 2),
                    column,
                )
                for dz, dx, dc in steps(depth, width, 2)
            ],
        ),
    )

    def give(stage, value):
        place_in = groups[stage][1]
        trace_out[stage] = value
        trace_in[stage, place_in] = value
        copies = []
        for k, partner in enumerate(groups[stage][2]):
            copies.append(
                pltpu.make_async_remote_copy(
                    src_ref=trace_out.at[stage],
                    dst_ref=trace_in.at[stage, place_in],
                    send_sem=trace_send.at[stage, k],
                    recv_sem=trace_recv.at[stage, k],
                    device_id=partner,
                    device_id_type=MESH,
                )
            )
            copies[-1].start()
        return copies

    def take(stage, copies):
        for copy in copies:
            copy.wait_recv()
        total = trace_in[stage, 0]
        for k in range(1, groups[stage][0]):
            total = total + trace_in[stage, k]
        return total

    first_copies = give(0, jnp.full((1, 128), trace, F32))
    square = 1.5 * once - 0.5 * apply(twice)
    once = apply(square)
    cube = 1.5 * once - 0.5 * apply(apply(once))
    last = 1.5 * first - 0.5 * cube
    for i in range(blocks):
        part = last[:, i * edge : (i + 1) * edge].T
        results[i] = 0.5 * (jnp.where(diagonal, 1.0, 0.0) - part) if i == 0 else -0.5 * part
    results[blocks] = jnp.zeros((edge, edge), F32)
    returns = []
    for r in (0, 2, 1):
        for k in range(BACK):
            if r == 1:
                back[1, k] = results[chosen[r][k]]
            else:
                going[r // 2, k] = results[chosen[r][k]]
        if r != 1:
            returns.append(
                pltpu.make_async_remote_copy(
                    src_ref=going.at[r // 2],
                    dst_ref=back.at[2 - r],
                    send_sem=back_send.at[r // 2],
                    recv_sem=back_recv.at[r // 2],
                    device_id=(near[r], column),
                    device_id_type=MESH,
                )
            )
            returns[-1].start()
    last_copies = give(1, take(0, first_copies))
    for copy in returns:
        copy.wait()
    weights = [
        [jnp.where(stored[r][k] == t, 1.0, 0.0).astype(F32) for r in range(3) for k in range(BACK)]
        for t in range(tiles_per)
    ]
    for at in range(0, edge, 8):
        pieces = [back[r, k, pl.ds(at, 8)] for r in range(3) for k in range(BACK)]
        for t in range(tiles_per):
            total = weights[t][0] * pieces[0]
            for weight, piece in zip(weights[t][1:], pieces[1:]):
                total = total + weight * piece
            out_ref[t, pl.ds(at, 8)] = total
    for copy in first_copies + last_copies:
        copy.wait_send()
    elec_ref[...] = jnp.broadcast_to(2.0 * take(1, last_copies), elec_ref.shape)


def on_device(ks_tiles, chem_shift, spectral_scale, sub_tiles, result_dest):
    owners = lax.axis_size("owner")
    columns = lax.axis_size("col")
    tiles_per, edge = ks_tiles.shape[0], ks_tiles.shape[1]
    blocks = sub_tiles.shape[1]
    order = blocks * edge
    widest = max(columns, owners)
    vmem, smem, hbm = pltpu.VMEM, pltpu.SMEM, pl.ANY
    dma = pltpu.SemaphoreType.DMA
    density, electrons = pl.pallas_call(
        functools.partial(kernel, owners, columns, blocks),
        out_shape=(
            jax.ShapeDtypeStruct((tiles_per, edge, edge), F32),
            jax.ShapeDtypeStruct((8, 128), F32),
        ),
        in_specs=[pl.BlockSpec(memory_space=vmem)] * 2 + [pl.BlockSpec(memory_space=hbm)] * 3,
        out_specs=[pl.BlockSpec(memory_space=vmem)] * 2,
        scratch_shapes=[
            vmem((tiles_per, edge, edge), BF16),
            vmem((blocks, blocks, owners * columns), jnp.int32),
            vmem((blocks, owners * columns), jnp.int32),
            vmem((3 * columns * ROOM, edge, edge), BF16),
            vmem((tiles_per, edge, edge), BF16),
            vmem((3 * columns * ROOM + 1, edge, edge), BF16),
            smem((blocks * blocks,), jnp.int32),
            vmem((order, order), BF16),
            vmem((order, order), BF16),
            vmem((blocks + 1, edge, edge), F32),
            vmem((2, BACK, edge, edge), F32),
            vmem((3, BACK, edge, edge), F32),
            vmem((2, 1, 128), F32),
            vmem((2, widest, 1, 128), F32),
            dma((3,)),
            dma((2,)),
            dma((3 * columns,)),
            dma((3 * columns,)),
            dma((2,)),
            dma((2,)),
            dma((2, widest)),
            dma((2, widest)),
            pltpu.SemaphoreType.REGULAR((2 + log2(owners),)),
        ],
        compiler_params=pltpu.CompilerParams(
            collective_id=0, has_side_effects=True, vmem_limit_bytes=48 * 2**20
        ),
        name="submatrix_density",
    )(
        chem_shift.reshape(1, 1),
        spectral_scale.reshape(1, 1),
        *(
            pltpu.with_memory_space_constraint(a, pltpu.HBM)
            for a in (
                ks_tiles,
                jnp.transpose(sub_tiles, (1, 2, 0)),
                result_dest.T,
            )
        )
    )
    return density, electrons[0, :1]


def solution(mesh):
    return jax.shard_map(
        on_device,
        mesh=mesh,
        in_specs=(P(("owner", "col"), None, None), P(), P(), P(), P()),
        out_specs=(P(("owner", "col"), None, None), P()),
        check_vma=False,
    )
```

```python
import functools
import itertools
import jax
import jax.numpy as jnp
from jax import lax
from jax.experimental import pallas as pl
from jax.experimental.pallas import tpu as pltpu
from jax.sharding import PartitionSpec as P

F32 = jnp.float32
BF16 = jnp.bfloat16
MESH = pl.DeviceIdType.MESH
ROOM = 2
BACK = 3
FAR = 1 << 20


def log2(n):
    assert n & (n - 1) == 0
    return n.bit_length() - 1


def dot(a, b):
    return jnp.dot(a, b, preferred_element_type=F32)


def kernel(
    owners, columns, blocks, chem_ref, scale_ref, tiles_hbm, sub_hbm, dest_hbm,
    out_ref, elec_ref, tiles_ref, lists, dests, packet, passing, arrived, place, high, low,
    results, going, back, trace_out, trace_in, fetch_sem, pass_sem, send_sem, recv_sem, back_send, back_recv,
    trace_send, trace_recv, ready,
):
    tiles_per, edge = tiles_ref.shape[0], tiles_ref.shape[1]
    devices = owners * columns
    owner = lax.axis_index("owner")
    column = lax.axis_index("col")
    myself = owner * columns + column
    tile_bits, column_bits = log2(tiles_per), log2(columns)
    near = [lax.rem(owner + owners + r - 1, owners) for r in range(3)]
    half = columns // 2
    core = owner & 1
    turn = 1 - 2 * core
    at = [lax.rem(column + turn * k + columns, columns) for k in range(columns)]
    before = at[columns - 1]

    fetches = [
        pltpu.make_async_copy(there, here, fetch_sem.at[n])
        for n, (there, here) in enumerate(
            (
                (sub_hbm, lists),
                (tiles_hbm, tiles_ref),
                (dest_hbm, dests),
            )
        )
    ]
    for fetch in fetches:
        fetch.start()
    beside = [(owner, at[1]), (owner, before), (near[0], column), (near[2], column)]
    barrier = pltpu.get_barrier_semaphore()

    def tell(sem, partners):
        for partner in partners:
            pl.semaphore_signal(sem, inc=1, device_id=partner, device_id_type=MESH)

    tell(barrier, beside)
    pl.semaphore_wait(barrier, len(beside))

    step = pltpu.make_async_remote_copy(
        src_ref=tiles_hbm,
        dst_ref=passing,
        send_sem=pass_sem.at[0],
        recv_sem=pass_sem.at[1],
        device_id=(owner, at[1]),
        device_id_type=MESH,
    )
    step.start()
    tell(ready.at[0], beside)
    for fetch in fetches:
        fetch.wait()

    shape = (blocks, devices)
    lane = lax.broadcasted_iota(jnp.int32, shape, 1)
    row = lax.broadcasted_iota(jnp.int32, shape, 0)

    def asked_of(source):
        least, most = jnp.full(shape, FAR, jnp.int32), jnp.full(shape, -1, jnp.int32)
        for i in range(blocks):
            asked = lists[i]
            mine = lax.shift_right_arithmetic(asked, tile_bits) == source
            code = (row + i * blocks) * tiles_per + (asked & (tiles_per - 1))
            least = jnp.minimum(least, jnp.where(mine, code, FAR))
            most = jnp.maximum(most, jnp.where(mine, code, -1))
        least = jnp.min(least, axis=0, keepdims=True) & (tiles_per - 1)
        most = jnp.max(most, axis=0, keepdims=True) & (tiles_per - 1)
        return least * tiles_per + most

    sends = []

    def pack(asked, tiles, r, to, ref, slot):
        both = jnp.sum(jnp.where(lane[:1] == near[r] * columns + to, asked, 0))
        ref[slot] = tiles[lax.shift_right_arithmetic(both, tile_bits)]
        ref[slot + 1] = tiles[both & (tiles_per - 1)]

    def send(asked, tiles, r, k, source, to):
        slot = (r * columns + k) * ROOM
        pack(asked, tiles, r, to, packet, slot)
        sends.append(
            pltpu.make_async_remote_copy(
                src_ref=packet.at[pl.ds(slot, ROOM)],
                dst_ref=arrived.at[pl.ds(((2 - r) * columns + source) * ROOM, ROOM)],
                send_sem=send_sem.at[r * columns + k],
                recv_sem=recv_sem.at[r * columns + k],
                device_id=(near[r], to),
                device_id_type=MESH,
            )
        )
        sends[-1].start()

    asked = asked_of(myself)
    pl.semaphore_wait(ready.at[0], len(beside))
    over = [(owner, at[2]), (owner, at[columns - 2])]
    tell(ready.at[1], over)
    for k in (columns - 1, 0):
        for r in range(3):
            if (r, k) != (1, 0):
                send(asked, tiles_ref, r, k, column, at[k])
    pl.semaphore_wait(ready.at[1], len(over))
    for k in range(columns - 2, half, -1):
        for r in range(3):
            send(asked, tiles_ref, r, k, column, at[k])
    pack(asked, tiles_ref, 1, column, arrived, (columns + column) * ROOM)
    asked = asked_of(owner * columns + before)

    nothing = 3 * columns * ROOM
    arrived[nothing] = jnp.zeros((edge, edge), BF16)
    across_i = lax.broadcasted_iota(jnp.int32, (blocks, blocks), 1)
    spot = across_i * blocks + lax.broadcasted_iota(jnp.int32, (blocks, blocks), 0)
    own = jnp.zeros((blocks, blocks), jnp.int32)
    for i in range(blocks):
        held = jnp.sum(jnp.where(lane == myself, lists[i], 0), axis=1, keepdims=True)
        own = own + jnp.where(across_i == i, held, 0)
    source = lax.shift_right_arithmetic(own, tile_bits)
    offset = lax.shift_right_arithmetic(source, column_bits) - owner + (owners + 1)
    offset = jnp.where(offset >= owners, offset - owners, offset)
    offset = jnp.where(offset >= owners, offset - owners, offset)
    base = (offset * columns + (source & (columns - 1))) * ROOM
    for p in range(blocks * blocks):
        here = spot == p
        entry = jnp.sum(jnp.where(here, own, 0))
        start = jnp.sum(jnp.where(here, base, 0))
        same = source == lax.shift_right_arithmetic(entry, tile_bits)
        rank = (jnp.min(jnp.where(same, spot, FAR)) < p).astype(jnp.int32)
        place[p] = jnp.where(entry >= 0, jnp.clip(start + rank, 0, nothing), nothing)

    step.wait()
    for k in range(half, 0, -1):
        for r in range(3):
            if (r, k) != (1, 1):
                send(asked, passing, r, k, before, at[k - 1])
    pack(asked, passing, 1, column, arrived, (columns + before) * ROOM)

    reach, stage = 1, 2
    while 2 * reach <= max(2, owners // 2):
        far = [
            (lax.rem(owner + reach, owners), column),
            (lax.rem(owner + owners - reach, owners), column),
        ]
        tell(ready.at[stage], far)
        pl.semaphore_wait(ready.at[stage], 2)
        reach, stage = 2 * reach, stage + 1

    targets = [
        [
            jnp.sum(jnp.where((lane == near[r] * columns + column) & (row == i), dests[...], 0))
            for i in range(blocks)
        ]
        for r in range(3)
    ]
    chosen = [[jnp.int32(blocks) for _ in range(BACK)] for _ in range(3)]
    stored = [[jnp.int32(-1) for _ in range(BACK)] for _ in range(3)]
    for r in range(3):
        taken = jnp.int32(0)
        sent = jnp.int32(0)
        for i in range(blocks):
            target = targets[r][i]
            home = lax.shift_right_arithmetic(target, tile_bits + column_bits)
            mine = (target >= 0) & (home == owner)
            for k in range(BACK):
                stored[r][k] = jnp.where(mine & (taken == k), target & (tiles_per - 1), stored[r][k])
            taken = taken + mine.astype(jnp.int32)
            target = targets[1][i]
            home = lax.shift_right_arithmetic(target, tile_bits + column_bits)
            theirs = (target >= 0) & (home == near[r])
            for k in range(BACK):
                chosen[r][k] = jnp.where(theirs & (sent == k), i, chosen[r][k])
            sent = sent + theirs.astype(jnp.int32)

    for copy in sends:
        copy.wait()

    chem = chem_ref[...]
    inverse = 1.0 / scale_ref[...]
    order = blocks * edge
    wide = 2 * edge
    diagonal = lax.broadcasted_iota(jnp.int32, (edge, edge), 0) == lax.broadcasted_iota(
        jnp.int32, (edge, edge), 1
    )
    parts = []
    for i, j in sorted(itertools.product(range(blocks), repeat=2), key=lambda p: (p[0] > 0, p[1])):
        part = arrived[place[i * blocks + j]].astype(F32)
        part = part + arrived[place[j * blocks + i]].T.astype(F32)
        part = part * (0.5 * inverse)
        if i == j:
            part = part - jnp.where(diagonal, chem * inverse, 0.0)
        rows, cols = pl.ds(i * edge, edge), pl.ds(j * edge, edge)
        upper = part.astype(BF16)
        high[rows, cols] = upper
        low[rows, cols] = (part - upper.astype(F32)).astype(BF16)
        if i == 0:
            parts.append(part)
    start = jnp.concatenate(parts, axis=1)

    def apply(u):
        upper = u.astype(BF16)
        lower = (u - upper.astype(F32)).astype(BF16)
        both = jnp.concatenate([upper, lower], axis=0)
        parts = []
        for at in range(0, order, wide):
            cut = pl.ds(at, wide)
            w = dot(both, high[:, cut])
            parts.append(w[:edge] + w[edge:] + dot(upper, low[:, cut]))
        return jnp.concatenate(parts, axis=1)

    first = 1.5 * start - 0.5 * apply(apply(start))
    once = apply(first)
    twice = apply(once)
    cubed = 1.5 * jnp.sum(first * once) - 0.5 * jnp.sum(once * twice)
    trace = 1.5 * jnp.sum(jnp.where(diagonal, first[:, :edge], 0.0)) - 0.5 * cubed
    trace = 0.5 * (edge - trace)

    inner = min(8, owners)
    width, depth = inner // 2, owners // inner
    here_x, here_z = lax.div(lax.rem(owner, inner), 2), lax.div(owner, inner)

    def steps(*sizes):
        every = list(itertools.product(*(range(size) for size in sizes)))[1:]
        return sorted(every, key=lambda p: -sum(min(n, size - n) for n, size in zip(p, sizes)))

    groups = (
        (
            2 * columns,
            core * columns + column,
            [
                (owner - core + lax.rem(core + dc, 2), lax.rem(column + dy, columns))
                for dy, dc in steps(columns, 2)
            ],
        ),
        (
            owners // 2,
            lax.div(owner, 2),
            [
                (
                    lax.rem(here_z + dz, depth) * inner + lax.rem(here_x + dx, width) * 2 + core,
                    column,
                )
                for dz, dx in steps(depth, width)
            ],
        ),
    )

    def give(stage, value):
        place_in = groups[stage][1]
        trace_out[stage] = value
        trace_in[stage, place_in] = value
        copies = []
        for k, partner in enumerate(groups[stage][2]):
            copies.append(
                pltpu.make_async_remote_copy(
                    src_ref=trace_out.at[stage],
                    dst_ref=trace_in.at[stage, place_in],
                    send_sem=trace_send.at[stage, k],
                    recv_sem=trace_recv.at[stage, k],
                    device_id=partner,
                    device_id_type=MESH,
                )
            )
            copies[-1].start()
        return copies

    def take(stage, copies):
        for copy in copies:
            copy.wait_recv()
        total = trace_in[stage, 0]
        for k in range(1, groups[stage][0]):
            total = total + trace_in[stage, k]
        return total

    first_copies = give(0, jnp.full((1, 128), trace, F32))
    square = 1.5 * once - 0.5 * apply(twice)
    once = apply(square)
    cube = 1.5 * once - 0.5 * apply(apply(once))
    last = 1.5 * first - 0.5 * cube
    for i in range(blocks):
        part = last[:, i * edge : (i + 1) * edge].T
        results[i] = 0.5 * (jnp.where(diagonal, 1.0, 0.0) - part) if i == 0 else -0.5 * part
    results[blocks] = jnp.zeros((edge, edge), F32)
    returns = []
    for r in (0, 2, 1):
        for k in range(BACK):
            if r == 1:
                back[1, k] = results[chosen[r][k]]
            else:
                going[r // 2, k] = results[chosen[r][k]]
        if r != 1:
            returns.append(
                pltpu.make_async_remote_copy(
                    src_ref=going.at[r // 2],
                    dst_ref=back.at[2 - r],
                    send_sem=back_send.at[r // 2],
                    recv_sem=back_recv.at[r // 2],
                    device_id=(near[r], column),
                    device_id_type=MESH,
                )
            )
            returns[-1].start()
    last_copies = give(1, take(0, first_copies))
    for copy in returns:
        copy.wait()
    weights = [
        [jnp.where(stored[r][k] == t, 1.0, 0.0).astype(F32) for r in range(3) for k in range(BACK)]
        for t in range(tiles_per)
    ]
    for at in range(0, edge, 8):
        pieces = [back[r, k, pl.ds(at, 8)] for r in range(3) for k in range(BACK)]
        for t in range(tiles_per):
            total = weights[t][0] * pieces[0]
            for weight, piece in zip(weights[t][1:], pieces[1:]):
                total = total + weight * piece
            out_ref[t, pl.ds(at, 8)] = total
    for copy in first_copies + last_copies:
        copy.wait_send()
    elec_ref[...] = jnp.broadcast_to(2.0 * take(1, last_copies), elec_ref.shape)


def on_device(ks_tiles, chem_shift, spectral_scale, sub_tiles, result_dest):
    owners = lax.axis_size("owner")
    columns = lax.axis_size("col")
    tiles_per, edge = ks_tiles.shape[0], ks_tiles.shape[1]
    blocks = sub_tiles.shape[1]
    order = blocks * edge
    widest = max(2 * columns, owners // 2)
    vmem, smem, hbm = pltpu.VMEM, pltpu.SMEM, pl.ANY
    dma = pltpu.SemaphoreType.DMA
    density, electrons = pl.pallas_call(
        functools.partial(kernel, owners, columns, blocks),
        out_shape=(
            jax.ShapeDtypeStruct((tiles_per, edge, edge), F32),
            jax.ShapeDtypeStruct((8, 128), F32),
        ),
        in_specs=[pl.BlockSpec(memory_space=vmem)] * 2 + [pl.BlockSpec(memory_space=hbm)] * 3,
        out_specs=[pl.BlockSpec(memory_space=vmem)] * 2,
        scratch_shapes=[
            vmem((tiles_per, edge, edge), BF16),
            vmem((blocks, blocks, owners * columns), jnp.int32),
            vmem((blocks, owners * columns), jnp.int32),
            vmem((3 * columns * ROOM, edge, edge), BF16),
            vmem((tiles_per, edge, edge), BF16),
            vmem((3 * columns * ROOM + 1, edge, edge), BF16),
            smem((blocks * blocks,), jnp.int32),
            vmem((order, order), BF16),
            vmem((order, order), BF16),
            vmem((blocks + 1, edge, edge), F32),
            vmem((2, BACK, edge, edge), F32),
            vmem((3, BACK, edge, edge), F32),
            vmem((2, 1, 128), F32),
            vmem((2, widest, 1, 128), F32),
            dma((3,)),
            dma((2,)),
            dma((3 * columns,)),
            dma((3 * columns,)),
            dma((2,)),
            dma((2,)),
            dma((2, widest)),
            dma((2, widest)),
            pltpu.SemaphoreType.REGULAR((2 + log2(owners),)),
        ],
        compiler_params=pltpu.CompilerParams(
            collective_id=0, has_side_effects=True, vmem_limit_bytes=48 * 2**20
        ),
        name="submatrix_density",
    )(
        chem_shift.reshape(1, 1),
        spectral_scale.reshape(1, 1),
        *(
            pltpu.with_memory_space_constraint(a, pltpu.HBM)
            for a in (
                ks_tiles,
                jnp.transpose(sub_tiles, (1, 2, 0)),
                result_dest.T,
            )
        )
    )
    return density, electrons[0, :1]


def solution(mesh):
    return jax.shard_map(
        on_device,
        mesh=mesh,
        in_specs=(P(("owner", "col"), None, None), P(), P(), P(), P()),
        out_specs=(P(("owner", "col"), None, None), P()),
        check_vma=False,
    )
```

```python
import functools
import itertools
import jax
import jax.numpy as jnp
from jax import lax
from jax.experimental import pallas as pl
from jax.experimental.pallas import tpu as pltpu
from jax.sharding import PartitionSpec as P

F32 = jnp.float32
BF16 = jnp.bfloat16
MESH = pl.DeviceIdType.MESH
ROOM = 2
BACK = 3
FAR = 1 << 20


def log2(n):
    assert n & (n - 1) == 0
    return n.bit_length() - 1


def dot(a, b):
    return jnp.dot(a, b, preferred_element_type=F32)


def kernel(
    owners, columns, blocks, chem_ref, scale_ref, tiles_hbm, sub_hbm, dest_hbm,
    out_ref, elec_ref, tiles_ref, lists, dests, packet, passing, arrived, place, high, low,
    results, going, back, trace_out, trace_in, fetch_sem, pass_sem, send_sem, recv_sem, back_send, back_recv,
    trace_send, trace_recv, ready,
):
    tiles_per, edge = tiles_ref.shape[0], tiles_ref.shape[1]
    devices = owners * columns
    owner = lax.axis_index("owner")
    column = lax.axis_index("col")
    myself = owner * columns + column
    tile_bits, column_bits = log2(tiles_per), log2(columns)
    near = [(owner + r - 1) & (owners - 1) for r in range(3)]
    half = columns // 2
    core = owner & 1
    turn = 1 - 2 * core
    at = [(column + turn * k) & (columns - 1) for k in range(columns)]
    before = at[columns - 1]

    beside = [(owner, at[1]), (owner, before), (near[0], column), (near[2], column)]
    barrier = pltpu.get_barrier_semaphore()

    def tell(sem, partners):
        for partner in partners:
            pl.semaphore_signal(sem, inc=1, device_id=partner, device_id_type=MESH)

    tell(barrier, beside)

    fetches = [
        pltpu.make_async_copy(there, here, fetch_sem.at[n])
        for n, (there, here) in enumerate(
            (
                (sub_hbm, lists),
                (tiles_hbm, tiles_ref),
                (dest_hbm, dests),
            )
        )
    ]
    for fetch in fetches:
        fetch.start()
    pl.semaphore_wait(barrier, len(beside))

    step = pltpu.make_async_remote_copy(
        src_ref=tiles_hbm,
        dst_ref=passing,
        send_sem=pass_sem.at[0],
        recv_sem=pass_sem.at[1],
        device_id=(owner, at[1]),
        device_id_type=MESH,
    )
    step.start()
    tell(ready.at[0], beside)
    for fetch in fetches:
        fetch.wait()

    shape = (blocks, devices)
    lane = lax.broadcasted_iota(jnp.int32, shape, 1)
    row = lax.broadcasted_iota(jnp.int32, shape, 0)

    def asked_of(source):
        least, most = jnp.full(shape, FAR, jnp.int32), jnp.full(shape, -1, jnp.int32)
        for i in range(blocks):
            asked = lists[i]
            mine = lax.shift_right_arithmetic(asked, tile_bits) == source
            code = (row + i * blocks) * tiles_per + (asked & (tiles_per - 1))
            least = jnp.minimum(least, jnp.where(mine, code, FAR))
            most = jnp.maximum(most, jnp.where(mine, code, -1))
        least = jnp.min(least, axis=0, keepdims=True) & (tiles_per - 1)
        most = jnp.max(most, axis=0, keepdims=True) & (tiles_per - 1)
        return least * tiles_per + most

    sends = []

    def pack(asked, tiles, r, to, ref, slot):
        both = jnp.sum(jnp.where(lane[:1] == near[r] * columns + to, asked, 0))
        ref[slot] = tiles[lax.shift_right_arithmetic(both, tile_bits)]
        ref[slot + 1] = tiles[both & (tiles_per - 1)]

    def send(asked, tiles, r, k, source, to):
        slot = (r * columns + k) * ROOM
        pack(asked, tiles, r, to, packet, slot)
        sends.append(
            pltpu.make_async_remote_copy(
                src_ref=packet.at[pl.ds(slot, ROOM)],
                dst_ref=arrived.at[pl.ds(((2 - r) * columns + source) * ROOM, ROOM)],
                send_sem=send_sem.at[r * columns + k],
                recv_sem=recv_sem.at[r * columns + k],
                device_id=(near[r], to),
                device_id_type=MESH,
            )
        )
        sends[-1].start()

    asked = asked_of(myself)
    pl.semaphore_wait(ready.at[0], len(beside))
    over = [(owner, at[2]), (owner, at[columns - 2])]
    tell(ready.at[1], over)
    for k in (columns - 1, 0):
        for r in range(3):
            if (r, k) != (1, 0):
                send(asked, tiles_ref, r, k, column, at[k])
    pl.semaphore_wait(ready.at[1], len(over))
    for k in range(columns - 2, half, -1):
        for r in range(3):
            send(asked, tiles_ref, r, k, column, at[k])
    pack(asked, tiles_ref, 1, column, arrived, (columns + column) * ROOM)
    asked = asked_of(owner * columns + before)

    step.wait_recv()
    for k in range(half, 0, -1):
        for r in range(3):
            if (r, k) != (1, 1):
                send(asked, passing, r, k, before, at[k - 1])
    pack(asked, passing, 1, column, arrived, (columns + before) * ROOM)

    reach, stage = 1, 2
    while 2 * reach <= max(2, owners // 2):
        far = [
            ((owner + reach) & (owners - 1), column),
            ((owner - reach) & (owners - 1), column),
        ]
        tell(ready.at[stage], far)
        pl.semaphore_wait(ready.at[stage], 2)
        reach, stage = 2 * reach, stage + 1

    nothing = 3 * columns * ROOM
    arrived[nothing] = jnp.zeros((edge, edge), BF16)
    across_i = lax.broadcasted_iota(jnp.int32, (blocks, blocks), 1)
    spot = across_i * blocks + lax.broadcasted_iota(jnp.int32, (blocks, blocks), 0)
    own = jnp.zeros((blocks, blocks), jnp.int32)
    for i in range(blocks):
        held = jnp.sum(jnp.where(lane == myself, lists[i], 0), axis=1, keepdims=True)
        own = own + jnp.where(across_i == i, held, 0)
    source = lax.shift_right_arithmetic(own, tile_bits)
    offset = lax.shift_right_arithmetic(source, column_bits) - owner + (owners + 1)
    offset = jnp.where(offset >= owners, offset - owners, offset)
    offset = jnp.where(offset >= owners, offset - owners, offset)
    base = (offset * columns + (source & (columns - 1))) * ROOM
    for p in range(blocks * blocks):
        here = spot == p
        entry = jnp.sum(jnp.where(here, own, 0))
        start = jnp.sum(jnp.where(here, base, 0))
        same = source == lax.shift_right_arithmetic(entry, tile_bits)
        rank = (jnp.min(jnp.where(same, spot, FAR)) < p).astype(jnp.int32)
        place[p] = jnp.where(entry >= 0, jnp.clip(start + rank, 0, nothing), nothing)

    targets = [
        [
            jnp.sum(jnp.where((lane == near[r] * columns + column) & (row == i), dests[...], 0))
            for i in range(blocks)
        ]
        for r in range(3)
    ]
    chosen = [[jnp.int32(blocks) for _ in range(BACK)] for _ in range(3)]
    stored = [[jnp.int32(-1) for _ in range(BACK)] for _ in range(3)]
    for r in range(3):
        taken = jnp.int32(0)
        sent = jnp.int32(0)
        for i in range(blocks):
            target = targets[r][i]
            home = lax.shift_right_arithmetic(target, tile_bits + column_bits)
            mine = (target >= 0) & (home == owner)
            for k in range(BACK):
                stored[r][k] = jnp.where(mine & (taken == k), target & (tiles_per - 1), stored[r][k])
            taken = taken + mine.astype(jnp.int32)
            target = targets[1][i]
            home = lax.shift_right_arithmetic(target, tile_bits + column_bits)
            theirs = (target >= 0) & (home == near[r])
            for k in range(BACK):
                chosen[r][k] = jnp.where(theirs & (sent == k), i, chosen[r][k])
            sent = sent + theirs.astype(jnp.int32)

    for copy in sends:
        copy.wait_recv()

    chem = chem_ref[...]
    inverse = 1.0 / scale_ref[...]
    order = blocks * edge
    wide = 2 * edge
    diagonal = lax.broadcasted_iota(jnp.int32, (edge, edge), 0) == lax.broadcasted_iota(
        jnp.int32, (edge, edge), 1
    )
    parts = []
    for i, j in sorted(itertools.product(range(blocks), repeat=2), key=lambda p: (p[0] > 0, p[1])):
        part = arrived[place[i * blocks + j]].astype(F32)
        part = part + arrived[place[j * blocks + i]].T.astype(F32)
        part = part * (0.5 * inverse)
        if i == j:
            part = part - jnp.where(diagonal, chem * inverse, 0.0)
        rows, cols = pl.ds(i * edge, edge), pl.ds(j * edge, edge)
        upper = part.astype(BF16)
        high[rows, cols] = upper
        low[rows, cols] = (part - upper.astype(F32)).astype(BF16)
        if i == 0:
            parts.append(part)
    start = jnp.concatenate(parts, axis=1)

    def apply(u):
        upper = u.astype(BF16)
        lower = (u - upper.astype(F32)).astype(BF16)
        both = jnp.concatenate([upper, lower], axis=0)
        parts = []
        for at in range(0, order, wide):
            cut = pl.ds(at, wide)
            w = dot(both, high[:, cut])
            parts.append(w[:edge] + w[edge:] + dot(upper, low[:, cut]))
        return jnp.concatenate(parts, axis=1)

    first = 1.5 * start - 0.5 * apply(apply(start))
    once = apply(first)
    twice = apply(once)
    cubed = 1.5 * jnp.sum(first * once) - 0.5 * jnp.sum(once * twice)
    trace = 1.5 * jnp.sum(jnp.where(diagonal, first[:, :edge], 0.0)) - 0.5 * cubed
    trace = 0.5 * (edge - trace)

    inner = min(8, owners)
    width, depth = inner // 2, owners // inner
    here_x = lax.shift_right_arithmetic(owner & (inner - 1), 1)
    here_z = lax.shift_right_arithmetic(owner, log2(inner))

    def steps(*sizes):
        every = list(itertools.product(*(range(size) for size in sizes)))[1:]
        return sorted(every, key=lambda p: -sum(min(n, size - n) for n, size in zip(p, sizes)))

    groups = (
        (
            2 * columns,
            core * columns + column,
            [
                (owner - core + ((core + dc) & 1), (column + dy) & (columns - 1))
                for dy, dc in steps(columns, 2)
            ],
        ),
        (
            owners // 2,
            lax.shift_right_arithmetic(owner, 1),
            [
                (
                    ((here_z + dz) & (depth - 1)) * inner + ((here_x + dx) & (width - 1)) * 2 + core,
                    column,
                )
                for dz, dx in steps(depth, width)
            ],
        ),
    )

    def give(stage, value):
        place_in = groups[stage][1]
        trace_out[stage] = value
        trace_in[stage, place_in] = value
        copies = []
        for k, partner in enumerate(groups[stage][2]):
            copies.append(
                pltpu.make_async_remote_copy(
                    src_ref=trace_out.at[stage],
                    dst_ref=trace_in.at[stage, place_in],
                    send_sem=trace_send.at[stage, k],
                    recv_sem=trace_recv.at[stage, k],
                    device_id=partner,
                    device_id_type=MESH,
                )
            )
            copies[-1].start()
        return copies

    def take(stage, copies):
        for copy in copies:
            copy.wait_recv()
        total = trace_in[stage, 0]
        for k in range(1, groups[stage][0]):
            total = total + trace_in[stage, k]
        return total

    first_copies = give(0, jnp.full((1, 128), trace, F32))
    square = 1.5 * once - 0.5 * apply(twice)
    once = apply(square)
    cube = 1.5 * once - 0.5 * apply(apply(once))
    last = 1.5 * first - 0.5 * cube
    for i in range(blocks):
        part = last[:, i * edge : (i + 1) * edge].T
        results[i] = 0.5 * (jnp.where(diagonal, 1.0, 0.0) - part) if i == 0 else -0.5 * part
    results[blocks] = jnp.zeros((edge, edge), F32)
    returns = []
    for r in (0, 2, 1):
        for k in range(BACK):
            if r == 1:
                back[1, k] = results[chosen[r][k]]
            else:
                going[r // 2, k] = results[chosen[r][k]]
        if r != 1:
            returns.append(
                pltpu.make_async_remote_copy(
                    src_ref=going.at[r // 2],
                    dst_ref=back.at[2 - r],
                    send_sem=back_send.at[r // 2],
                    recv_sem=back_recv.at[r // 2],
                    device_id=(near[r], column),
                    device_id_type=MESH,
                )
            )
            returns[-1].start()
    last_copies = give(1, take(0, first_copies))
    for copy in returns:
        copy.wait()
    weights = [
        [jnp.where(stored[r][k] == t, 1.0, 0.0).astype(F32) for r in range(3) for k in range(BACK)]
        for t in range(tiles_per)
    ]
    for at in range(0, edge, 8):
        pieces = [back[r, k, pl.ds(at, 8)] for r in range(3) for k in range(BACK)]
        for t in range(tiles_per):
            total = weights[t][0] * pieces[0]
            for weight, piece in zip(weights[t][1:], pieces[1:]):
                total = total + weight * piece
            out_ref[t, pl.ds(at, 8)] = total
    for copy in [step, *sends, *first_copies, *last_copies]:
        copy.wait_send()
    elec_ref[...] = jnp.broadcast_to(2.0 * take(1, last_copies), elec_ref.shape)


def on_device(ks_tiles, chem_shift, spectral_scale, sub_tiles, result_dest):
    owners = lax.axis_size("owner")
    columns = lax.axis_size("col")
    tiles_per, edge = ks_tiles.shape[0], ks_tiles.shape[1]
    blocks = sub_tiles.shape[1]
    order = blocks * edge
    widest = max(2 * columns, owners // 2)
    vmem, smem, hbm = pltpu.VMEM, pltpu.SMEM, pl.ANY
    dma = pltpu.SemaphoreType.DMA
    density, electrons = pl.pallas_call(
        functools.partial(kernel, owners, columns, blocks),
        out_shape=(
            jax.ShapeDtypeStruct((tiles_per, edge, edge), F32),
            jax.ShapeDtypeStruct((8, 128), F32),
        ),
        in_specs=[pl.BlockSpec(memory_space=vmem)] * 2 + [pl.BlockSpec(memory_space=hbm)] * 3,
        out_specs=[pl.BlockSpec(memory_space=vmem)] * 2,
        scratch_shapes=[
            vmem((tiles_per, edge, edge), BF16),
            vmem((blocks, blocks, owners * columns), jnp.int32),
            vmem((blocks, owners * columns), jnp.int32),
            vmem((3 * columns * ROOM, edge, edge), BF16),
            vmem((tiles_per, edge, edge), BF16),
            vmem((3 * columns * ROOM + 1, edge, edge), BF16),
            smem((blocks * blocks,), jnp.int32),
            vmem((order, order), BF16),
            vmem((order, order), BF16),
            vmem((blocks + 1, edge, edge), F32),
            vmem((2, BACK, edge, edge), F32),
            vmem((3, BACK, edge, edge), F32),
            vmem((2, 1, 128), F32),
            vmem((2, widest, 1, 128), F32),
            dma((3,)),
            dma((2,)),
            dma((3 * columns,)),
            dma((3 * columns,)),
            dma((2,)),
            dma((2,)),
            dma((2, widest)),
            dma((2, widest)),
            pltpu.SemaphoreType.REGULAR((2 + log2(owners),)),
        ],
        compiler_params=pltpu.CompilerParams(
            collective_id=0, has_side_effects=True, vmem_limit_bytes=48 * 2**20
        ),
        name="submatrix_density",
    )(
        chem_shift.reshape(1, 1),
        spectral_scale.reshape(1, 1),
        *(
            pltpu.with_memory_space_constraint(a, pltpu.HBM)
            for a in (
                ks_tiles,
                jnp.transpose(sub_tiles, (1, 2, 0)),
                result_dest.T,
            )
        )
    )
    return density, electrons[0, :1]


def solution(mesh):
    return jax.shard_map(
        on_device,
        mesh=mesh,
        in_specs=(P(("owner", "col"), None, None), P(), P(), P(), P()),
        out_specs=(P(("owner", "col"), None, None), P()),
        check_vma=False,
    )
```

```python
import functools
import itertools
import jax
import jax.numpy as jnp
from jax import lax
from jax.experimental import pallas as pl
from jax.experimental.pallas import tpu as pltpu
from jax.sharding import PartitionSpec as P

F32 = jnp.float32
BF16 = jnp.bfloat16
MESH = pl.DeviceIdType.MESH
ROOM = 2
BACK = 3
FAR = 1 << 20


def log2(n):
    assert n & (n - 1) == 0
    return n.bit_length() - 1


def dot(a, b):
    return jnp.dot(a, b, preferred_element_type=F32)


def kernel(
    owners, columns, blocks, chem_ref, scale_ref, tiles_hbm, sub_hbm, dest_hbm,
    out_ref, elec_ref, tiles_ref, lists, dests, packet, passing, arrived, place, high, low,
    results, going, back, trace_out, trace_in, fetch_sem, pass_sem, send_sem, recv_sem, back_send, back_recv,
    trace_send, trace_recv, ready,
):
    tiles_per, edge = tiles_ref.shape[0], tiles_ref.shape[1]
    devices = owners * columns
    owner = lax.axis_index("owner")
    column = lax.axis_index("col")
    myself = owner * columns + column
    tile_bits, column_bits = log2(tiles_per), log2(columns)
    near = [(owner + r - 1) & (owners - 1) for r in range(3)]
    half = columns // 2
    core = owner & 1
    turn = 1 - 2 * core
    at = [(column + turn * k) & (columns - 1) for k in range(columns)]
    before = at[columns - 1]

    beside = [(owner, at[1]), (owner, before), (near[0], column), (near[2], column)]
    barrier = pltpu.get_barrier_semaphore()

    def tell(sem, partners):
        for partner in partners:
            pl.semaphore_signal(sem, inc=1, device_id=partner, device_id_type=MESH)

    tell(barrier, beside)

    fetches = [
        pltpu.make_async_copy(there, here, fetch_sem.at[n])
        for n, (there, here) in enumerate(
            (
                (sub_hbm, lists),
                (tiles_hbm, tiles_ref),
                (dest_hbm, dests),
            )
        )
    ]
    for fetch in fetches:
        fetch.start()
    pl.semaphore_wait(barrier, len(beside))

    step = pltpu.make_async_remote_copy(
        src_ref=tiles_hbm,
        dst_ref=passing,
        send_sem=pass_sem.at[0],
        recv_sem=pass_sem.at[1],
        device_id=(owner, at[1]),
        device_id_type=MESH,
    )
    step.start()
    tell(ready.at[0], beside)
    for fetch in fetches:
        fetch.wait()

    shape = (blocks, devices)
    lane = lax.broadcasted_iota(jnp.int32, shape, 1)
    row = lax.broadcasted_iota(jnp.int32, shape, 0)

    def asked_of(source):
        least, most = jnp.full(shape, FAR, jnp.int32), jnp.full(shape, -1, jnp.int32)
        for i in range(blocks):
            asked = lists[i]
            mine = lax.shift_right_arithmetic(asked, tile_bits) == source
            code = (row + i * blocks) * tiles_per + (asked & (tiles_per - 1))
            least = jnp.minimum(least, jnp.where(mine, code, FAR))
            most = jnp.maximum(most, jnp.where(mine, code, -1))
        least = jnp.min(least, axis=0, keepdims=True) & (tiles_per - 1)
        most = jnp.max(most, axis=0, keepdims=True) & (tiles_per - 1)
        return least * tiles_per + most

    sends = []

    def pack(asked, tiles, r, to, ref, slot):
        both = jnp.sum(jnp.where(lane[:1] == near[r] * columns + to, asked, 0))
        ref[slot] = tiles[lax.shift_right_arithmetic(both, tile_bits)]
        ref[slot + 1] = tiles[both & (tiles_per - 1)]

    def send(asked, tiles, r, k, source, to):
        slot = (r * columns + k) * ROOM
        pack(asked, tiles, r, to, packet, slot)
        sends.append(
            pltpu.make_async_remote_copy(
                src_ref=packet.at[pl.ds(slot, ROOM)],
                dst_ref=arrived.at[pl.ds(((2 - r) * columns + source) * ROOM, ROOM)],
                send_sem=send_sem.at[r * columns + k],
                recv_sem=recv_sem.at[r * columns + k],
                device_id=(near[r], to),
                device_id_type=MESH,
            )
        )
        sends[-1].start()

    asked = asked_of(myself)
    pl.semaphore_wait(ready.at[0], len(beside))
    over = [(owner, at[2]), (owner, at[columns - 2])]
    tell(ready.at[1], over)
    for k in (columns - 1, 0):
        for r in range(3):
            if (r, k) != (1, 0):
                send(asked, tiles_ref, r, k, column, at[k])
    pl.semaphore_wait(ready.at[1], len(over))
    for k in range(columns - 2, half, -1):
        for r in range(3):
            send(asked, tiles_ref, r, k, column, at[k])
    pack(asked, tiles_ref, 1, column, arrived, (columns + column) * ROOM)
    asked = asked_of(owner * columns + before)

    nothing = 3 * columns * ROOM
    arrived[nothing] = jnp.zeros((edge, edge), BF16)
    across_i = lax.broadcasted_iota(jnp.int32, (blocks, blocks), 1)
    spot = across_i * blocks + lax.broadcasted_iota(jnp.int32, (blocks, blocks), 0)
    own = jnp.zeros((blocks, blocks), jnp.int32)
    for i in range(blocks):
        held = jnp.sum(jnp.where(lane == myself, lists[i], 0), axis=1, keepdims=True)
        own = own + jnp.where(across_i == i, held, 0)
    source = lax.shift_right_arithmetic(own, tile_bits)
    offset = lax.shift_right_arithmetic(source, column_bits) - owner + (owners + 1)
    offset = jnp.where(offset >= owners, offset - owners, offset)
    offset = jnp.where(offset >= owners, offset - owners, offset)
    base = (offset * columns + (source & (columns - 1))) * ROOM
    for p in range(blocks * blocks):
        here = spot == p
        entry = jnp.sum(jnp.where(here, own, 0))
        start = jnp.sum(jnp.where(here, base, 0))
        same = source == lax.shift_right_arithmetic(entry, tile_bits)
        rank = (jnp.min(jnp.where(same, spot, FAR)) < p).astype(jnp.int32)
        place[p] = jnp.where(entry >= 0, jnp.clip(start + rank, 0, nothing), nothing)

    step.wait_recv()
    for k in range(half, 0, -1):
        for r in range(3):
            if (r, k) != (1, 1):
                send(asked, passing, r, k, before, at[k - 1])
    pack(asked, passing, 1, column, arrived, (columns + before) * ROOM)

    reach, stage = 1, 2
    while 2 * reach <= max(2, owners // 2):
        far = [
            ((owner + reach) & (owners - 1), column),
            ((owner - reach) & (owners - 1), column),
        ]
        tell(ready.at[stage], far)
        pl.semaphore_wait(ready.at[stage], 2)
        reach, stage = 2 * reach, stage + 1

    targets = [
        [
            jnp.sum(jnp.where((lane == near[r] * columns + column) & (row == i), dests[...], 0))
            for i in range(blocks)
        ]
        for r in range(3)
    ]
    chosen = [[jnp.int32(blocks) for _ in range(BACK)] for _ in range(3)]
    stored = [[jnp.int32(-1) for _ in range(BACK)] for _ in range(3)]
    for r in range(3):
        taken = jnp.int32(0)
        sent = jnp.int32(0)
        for i in range(blocks):
            target = targets[r][i]
            home = lax.shift_right_arithmetic(target, tile_bits + column_bits)
            mine = (target >= 0) & (home == owner)
            for k in range(BACK):
                stored[r][k] = jnp.where(mine & (taken == k), target & (tiles_per - 1), stored[r][k])
            taken = taken + mine.astype(jnp.int32)
            target = targets[1][i]
            home = lax.shift_right_arithmetic(target, tile_bits + column_bits)
            theirs = (target >= 0) & (home == near[r])
            for k in range(BACK):
                chosen[r][k] = jnp.where(theirs & (sent == k), i, chosen[r][k])
            sent = sent + theirs.astype(jnp.int32)

    for copy in sends:
        copy.wait_recv()

    chem = chem_ref[...]
    inverse = 1.0 / scale_ref[...]
    order = blocks * edge
    wide = 2 * edge
    diagonal = lax.broadcasted_iota(jnp.int32, (edge, edge), 0) == lax.broadcasted_iota(
        jnp.int32, (edge, edge), 1
    )
    parts = []
    for i, j in sorted(itertools.product(range(blocks), repeat=2), key=lambda p: (p[0] > 0, p[1])):
        part = arrived[place[i * blocks + j]].astype(F32)
        part = part + arrived[place[j * blocks + i]].T.astype(F32)
        part = part * (0.5 * inverse)
        if i == j:
            part = part - jnp.where(diagonal, chem * inverse, 0.0)
        rows, cols = pl.ds(i * edge, edge), pl.ds(j * edge, edge)
        upper = part.astype(BF16)
        high[rows, cols] = upper
        low[rows, cols] = (part - upper.astype(F32)).astype(BF16)
        if i == 0:
            parts.append(part)
    start = jnp.concatenate(parts, axis=1)

    def apply(u):
        upper = u.astype(BF16)
        lower = (u - upper.astype(F32)).astype(BF16)
        both = jnp.concatenate([upper, lower], axis=0)
        parts = []
        for at in range(0, order, wide):
            cut = pl.ds(at, wide)
            w = dot(both, high[:, cut])
            parts.append(w[:edge] + w[edge:] + dot(upper, low[:, cut]))
        return jnp.concatenate(parts, axis=1)

    first = 1.5 * start - 0.5 * apply(apply(start))
    once = apply(first)
    twice = apply(once)
    cubed = 1.5 * jnp.sum(first * once) - 0.5 * jnp.sum(once * twice)
    trace = 1.5 * jnp.sum(jnp.where(diagonal, first[:, :edge], 0.0)) - 0.5 * cubed
    trace = 0.5 * (edge - trace)

    inner = min(8, owners)
    width, depth = inner // 2, owners // inner
    here_x = lax.shift_right_arithmetic(owner & (inner - 1), 1)
    here_z = lax.shift_right_arithmetic(owner, log2(inner))

    def steps(*sizes):
        every = list(itertools.product(*(range(size) for size in sizes)))[1:]
        return sorted(every, key=lambda p: -sum(min(n, size - n) for n, size in zip(p, sizes)))

    groups = (
        (
            2 * columns,
            core * columns + column,
            [
                (owner - core + ((core + dc) & 1), (column + dy) & (columns - 1))
                for dy, dc in steps(columns, 2)
            ],
        ),
        (
            owners // 2,
            lax.shift_right_arithmetic(owner, 1),
            [
                (
                    ((here_z + dz) & (depth - 1)) * inner + ((here_x + dx) & (width - 1)) * 2 + core,
                    column,
                )
                for dz, dx in steps(depth, width)
            ],
        ),
    )

    def give(stage, value):
        place_in = groups[stage][1]
        trace_out[stage] = value
        trace_in[stage, place_in] = value
        copies = []
        for k, partner in enumerate(groups[stage][2]):
            copies.append(
                pltpu.make_async_remote_copy(
                    src_ref=trace_out.at[stage],
                    dst_ref=trace_in.at[stage, place_in],
                    send_sem=trace_send.at[stage, k],
                    recv_sem=trace_recv.at[stage, k],
                    device_id=partner,
                    device_id_type=MESH,
                )
            )
            copies[-1].start()
        return copies

    def take(stage, copies):
        for copy in copies:
            copy.wait_recv()
        total = trace_in[stage, 0]
        for k in range(1, groups[stage][0]):
            total = total + trace_in[stage, k]
        return total

    first_copies = give(0, jnp.full((1, 128), trace, F32))
    square = 1.5 * once - 0.5 * apply(twice)
    once = apply(square)
    cube = 1.5 * once - 0.5 * apply(apply(once))
    last = 1.5 * first - 0.5 * cube
    for i in range(blocks):
        part = last[:, i * edge : (i + 1) * edge].T
        results[i] = 0.5 * (jnp.where(diagonal, 1.0, 0.0) - part) if i == 0 else -0.5 * part
    results[blocks] = jnp.zeros((edge, edge), F32)
    returns = []
    for r in (0, 2, 1):
        for k in range(BACK):
            if r == 1:
                back[1, k] = results[chosen[r][k]]
            else:
                going[r // 2, k] = results[chosen[r][k]]
        if r != 1:
            returns.append(
                pltpu.make_async_remote_copy(
                    src_ref=going.at[r // 2],
                    dst_ref=back.at[2 - r],
                    send_sem=back_send.at[r // 2],
                    recv_sem=back_recv.at[r // 2],
                    device_id=(near[r], column),
                    device_id_type=MESH,
                )
            )
            returns[-1].start()
    last_copies = give(1, take(0, first_copies))
    for copy in returns:
        copy.wait()
    weights = [
        [jnp.where(stored[r][k] == t, 1.0, 0.0).astype(F32) for r in range(3) for k in range(BACK)]
        for t in range(tiles_per)
    ]
    for at in range(0, edge, 8):
        pieces = [back[r, k, pl.ds(at, 8)] for r in range(3) for k in range(BACK)]
        for t in range(tiles_per):
            total = weights[t][0] * pieces[0]
            for weight, piece in zip(weights[t][1:], pieces[1:]):
                total = total + weight * piece
            out_ref[t, pl.ds(at, 8)] = total
    for copy in [step, *sends, *first_copies, *last_copies]:
        copy.wait_send()
    elec_ref[...] = jnp.broadcast_to(2.0 * take(1, last_copies), elec_ref.shape)


def on_device(ks_tiles, chem_shift, spectral_scale, sub_tiles, result_dest):
    owners = lax.axis_size("owner")
    columns = lax.axis_size("col")
    tiles_per, edge = ks_tiles.shape[0], ks_tiles.shape[1]
    blocks = sub_tiles.shape[1]
    order = blocks * edge
    widest = max(2 * columns, owners // 2)
    vmem, smem, hbm = pltpu.VMEM, pltpu.SMEM, pl.ANY
    dma = pltpu.SemaphoreType.DMA
    density, electrons = pl.pallas_call(
        functools.partial(kernel, owners, columns, blocks),
        out_shape=(
            jax.ShapeDtypeStruct((tiles_per, edge, edge), F32),
            jax.ShapeDtypeStruct((8, 128), F32),
        ),
        in_specs=[pl.BlockSpec(memory_space=vmem)] * 2 + [pl.BlockSpec(memory_space=hbm)] * 3,
        out_specs=[pl.BlockSpec(memory_space=vmem)] * 2,
        scratch_shapes=[
            vmem((tiles_per, edge, edge), BF16),
            vmem((blocks, blocks, owners * columns), jnp.int32),
            vmem((blocks, owners * columns), jnp.int32),
            vmem((3 * columns * ROOM, edge, edge), BF16),
            vmem((tiles_per, edge, edge), BF16),
            vmem((3 * columns * ROOM + 1, edge, edge), BF16),
            smem((blocks * blocks,), jnp.int32),
            vmem((order, order), BF16),
            vmem((order, order), BF16),
            vmem((blocks + 1, edge, edge), F32),
            vmem((2, BACK, edge, edge), F32),
            vmem((3, BACK, edge, edge), F32),
            vmem((2, 1, 128), F32),
            vmem((2, widest, 1, 128), F32),
            dma((3,)),
            dma((2,)),
            dma((3 * columns,)),
            dma((3 * columns,)),
            dma((2,)),
            dma((2,)),
            dma((2, widest)),
            dma((2, widest)),
            pltpu.SemaphoreType.REGULAR((2 + log2(owners),)),
        ],
        compiler_params=pltpu.CompilerParams(
            collective_id=0, has_side_effects=True, vmem_limit_bytes=48 * 2**20
        ),
        name="submatrix_density",
    )(
        chem_shift.reshape(1, 1),
        spectral_scale.reshape(1, 1),
        *(
            pltpu.with_memory_space_constraint(a, pltpu.HBM)
            for a in (
                ks_tiles,
                jnp.transpose(sub_tiles, (1, 2, 0)),
                result_dest.T,
            )
        )
    )
    return density, electrons[0, :1]


def solution(mesh):
    return jax.shard_map(
        on_device,
        mesh=mesh,
        in_specs=(P(("owner", "col"), None, None), P(), P(), P(), P()),
        out_specs=(P(("owner", "col"), None, None), P()),
        check_vma=False,
    )
```

```python
import functools
import itertools
import jax
import jax.numpy as jnp
from jax import lax
from jax.experimental import pallas as pl
from jax.experimental.pallas import tpu as pltpu
from jax.sharding import PartitionSpec as P

F32 = jnp.float32
BF16 = jnp.bfloat16
MESH = pl.DeviceIdType.MESH
ROOM = 2
BACK = 3
FAR = 1 << 20


def log2(n):
    assert n & (n - 1) == 0
    return n.bit_length() - 1


def dot(a, b):
    return jnp.dot(a, b, preferred_element_type=F32)


def kernel(
    owners, columns, blocks, chem_ref, scale_ref, tiles_hbm, sub_hbm, dest_hbm,
    out_ref, elec_ref, tiles_ref, lists, dests, packet, passing, arrived, place, high, low,
    results, going, back, trace_out, trace_in, fetch_sem, pass_sem, send_sem, recv_sem, back_send, back_recv,
    trace_send, trace_recv, ready,
):
    tiles_per, edge = tiles_ref.shape[0], tiles_ref.shape[1]
    devices = owners * columns
    owner = lax.axis_index("owner")
    column = lax.axis_index("col")
    myself = owner * columns + column
    tile_bits, column_bits = log2(tiles_per), log2(columns)
    near = [lax.rem(owner + owners + r - 1, owners) for r in range(3)]
    half = columns // 2
    core = owner & 1
    turn = 1 - 2 * core
    at = [lax.rem(column + turn * k + columns, columns) for k in range(columns)]
    before = at[columns - 1]

    fetches = [
        pltpu.make_async_copy(there, here, fetch_sem.at[n])
        for n, (there, here) in enumerate(
            (
                (sub_hbm, lists),
                (tiles_hbm, tiles_ref),
                (dest_hbm, dests),
            )
        )
    ]
    for fetch in fetches:
        fetch.start()
    beside = [(owner, at[1]), (owner, before), (near[0], column), (near[2], column)]
    barrier = pltpu.get_barrier_semaphore()

    def tell(sem, partners):
        for partner in partners:
            pl.semaphore_signal(sem, inc=1, device_id=partner, device_id_type=MESH)

    tell(barrier, beside)
    pl.semaphore_wait(barrier, len(beside))

    step = pltpu.make_async_remote_copy(
        src_ref=tiles_hbm,
        dst_ref=passing,
        send_sem=pass_sem.at[0],
        recv_sem=pass_sem.at[1],
        device_id=(owner, at[1]),
        device_id_type=MESH,
    )
    step.start()
    tell(ready.at[0], beside)
    for fetch in fetches:
        fetch.wait()

    shape = (blocks, devices)
    lane = lax.broadcasted_iota(jnp.int32, shape, 1)
    row = lax.broadcasted_iota(jnp.int32, shape, 0)

    def asked_of(source):
        least, most = jnp.full(shape, FAR, jnp.int32), jnp.full(shape, -1, jnp.int32)
        for i in range(blocks):
            asked = lists[i]
            mine = lax.shift_right_arithmetic(asked, tile_bits) == source
            code = (row + i * blocks) * tiles_per + (asked & (tiles_per - 1))
            least = jnp.minimum(least, jnp.where(mine, code, FAR))
            most = jnp.maximum(most, jnp.where(mine, code, -1))
        least = jnp.min(least, axis=0, keepdims=True) & (tiles_per - 1)
        most = jnp.max(most, axis=0, keepdims=True) & (tiles_per - 1)
        return least * tiles_per + most

    sends = []

    def pack(asked, tiles, r, to, ref, slot):
        both = jnp.sum(jnp.where(lane[:1] == near[r] * columns + to, asked, 0))
        ref[slot] = tiles[lax.shift_right_arithmetic(both, tile_bits)]
        ref[slot + 1] = tiles[both & (tiles_per - 1)]

    def send(asked, tiles, r, k, source, to):
        slot = (r * columns + k) * ROOM
        pack(asked, tiles, r, to, packet, slot)
        sends.append(
            pltpu.make_async_remote_copy(
                src_ref=packet.at[pl.ds(slot, ROOM)],
                dst_ref=arrived.at[pl.ds(((2 - r) * columns + source) * ROOM, ROOM)],
                send_sem=send_sem.at[r * columns + k],
                recv_sem=recv_sem.at[r * columns + k],
                device_id=(near[r], to),
                device_id_type=MESH,
            )
        )
        sends[-1].start()

    asked = asked_of(myself)
    pl.semaphore_wait(ready.at[0], len(beside))
    over = [(owner, at[2]), (owner, at[columns - 2])]
    tell(ready.at[1], over)
    for k in (columns - 1, 0):
        for r in range(3):
            if (r, k) != (1, 0):
                send(asked, tiles_ref, r, k, column, at[k])
    pl.semaphore_wait(ready.at[1], len(over))
    for k in range(columns - 2, half, -1):
        for r in range(3):
            send(asked, tiles_ref, r, k, column, at[k])
    pack(asked, tiles_ref, 1, column, arrived, (columns + column) * ROOM)
    asked = asked_of(owner * columns + before)

    nothing = 3 * columns * ROOM
    arrived[nothing] = jnp.zeros((edge, edge), BF16)
    across_i = lax.broadcasted_iota(jnp.int32, (blocks, blocks), 1)
    spot = across_i * blocks + lax.broadcasted_iota(jnp.int32, (blocks, blocks), 0)
    own = jnp.zeros((blocks, blocks), jnp.int32)
    for i in range(blocks):
        held = jnp.sum(jnp.where(lane == myself, lists[i], 0), axis=1, keepdims=True)
        own = own + jnp.where(across_i == i, held, 0)
    source = lax.shift_right_arithmetic(own, tile_bits)
    offset = lax.shift_right_arithmetic(source, column_bits) - owner + (owners + 1)
    offset = jnp.where(offset >= owners, offset - owners, offset)
    offset = jnp.where(offset >= owners, offset - owners, offset)
    base = (offset * columns + (source & (columns - 1))) * ROOM
    for p in range(blocks * blocks):
        here = spot == p
        entry = jnp.sum(jnp.where(here, own, 0))
        start = jnp.sum(jnp.where(here, base, 0))
        same = source == lax.shift_right_arithmetic(entry, tile_bits)
        rank = (jnp.min(jnp.where(same, spot, FAR)) < p).astype(jnp.int32)
        place[p] = jnp.where(entry >= 0, jnp.clip(start + rank, 0, nothing), nothing)

    targets = [
        [
            jnp.sum(jnp.where((lane == near[r] * columns + column) & (row == i), dests[...], 0))
            for i in range(blocks)
        ]
        for r in range(3)
    ]
    chosen = [[jnp.int32(blocks) for _ in range(BACK)] for _ in range(3)]
    stored = [[jnp.int32(-1) for _ in range(BACK)] for _ in range(3)]
    for r in range(3):
        taken = jnp.int32(0)
        sent = jnp.int32(0)
        for i in range(blocks):
            target = targets[r][i]
            home = lax.shift_right_arithmetic(target, tile_bits + column_bits)
            mine = (target >= 0) & (home == owner)
            for k in range(BACK):
                stored[r][k] = jnp.where(mine & (taken == k), target & (tiles_per - 1), stored[r][k])
            taken = taken + mine.astype(jnp.int32)
            target = targets[1][i]
            home = lax.shift_right_arithmetic(target, tile_bits + column_bits)
            theirs = (target >= 0) & (home == near[r])
            for k in range(BACK):
                chosen[r][k] = jnp.where(theirs & (sent == k), i, chosen[r][k])
            sent = sent + theirs.astype(jnp.int32)

    step.wait()
    for k in range(half, 0, -1):
        for r in range(3):
            if (r, k) != (1, 1):
                send(asked, passing, r, k, before, at[k - 1])
    pack(asked, passing, 1, column, arrived, (columns + before) * ROOM)

    reaches = [1]
    while 4 * reaches[-1] <= owners // 2:
        reaches.append(2 * reaches[-1])
    final = len(reaches) + 1
    for stage, reach in enumerate(reaches, 2):
        far = [
            (lax.rem(owner + reach, owners), column),
            (lax.rem(owner + owners - reach, owners), column),
        ]
        tell(ready.at[stage], far)
        if stage < final:
            pl.semaphore_wait(ready.at[stage], 2)

    for copy in sends:
        copy.wait()

    chem = chem_ref[...]
    inverse = 1.0 / scale_ref[...]
    order = blocks * edge
    wide = 2 * edge
    diagonal = lax.broadcasted_iota(jnp.int32, (edge, edge), 0) == lax.broadcasted_iota(
        jnp.int32, (edge, edge), 1
    )
    parts = []
    for i, j in sorted(itertools.product(range(blocks), repeat=2), key=lambda p: (p[0] > 0, p[1])):
        part = arrived[place[i * blocks + j]].astype(F32)
        part = part + arrived[place[j * blocks + i]].T.astype(F32)
        part = part * (0.5 * inverse)
        if i == j:
            part = part - jnp.where(diagonal, chem * inverse, 0.0)
        rows, cols = pl.ds(i * edge, edge), pl.ds(j * edge, edge)
        upper = part.astype(BF16)
        high[rows, cols] = upper
        low[rows, cols] = (part - upper.astype(F32)).astype(BF16)
        if i == 0:
            parts.append(part)
    start = jnp.concatenate(parts, axis=1)

    def apply(u):
        upper = u.astype(BF16)
        lower = (u - upper.astype(F32)).astype(BF16)
        both = jnp.concatenate([upper, lower], axis=0)
        parts = []
        for at in range(0, order, wide):
            cut = pl.ds(at, wide)
            w = dot(both, high[:, cut])
            parts.append(w[:edge] + w[edge:] + dot(upper, low[:, cut]))
        return jnp.concatenate(parts, axis=1)

    first = 1.5 * start - 0.5 * apply(apply(start))
    once = apply(first)
    twice = apply(once)
    cubed = 1.5 * jnp.sum(first * once) - 0.5 * jnp.sum(once * twice)
    trace = 1.5 * jnp.sum(jnp.where(diagonal, first[:, :edge], 0.0)) - 0.5 * cubed
    trace = 0.5 * (edge - trace)

    inner = min(8, owners)
    width, depth = inner // 2, owners // inner
    here_x, here_z = lax.div(lax.rem(owner, inner), 2), lax.div(owner, inner)

    def steps(*sizes):
        every = list(itertools.product(*(range(size) for size in sizes)))[1:]
        return sorted(every, key=lambda p: -sum(min(n, size - n) for n, size in zip(p, sizes)))

    groups = (
        (
            2 * columns,
            core * columns + column,
            [
                (owner - core + lax.rem(core + dc, 2), lax.rem(column + dy, columns))
                for dy, dc in steps(columns, 2)
            ],
        ),
        (
            owners // 2,
            lax.div(owner, 2),
            [
                (
                    lax.rem(here_z + dz, depth) * inner + lax.rem(here_x + dx, width) * 2 + core,
                    column,
                )
                for dz, dx in steps(depth, width)
            ],
        ),
    )

    def give(stage, value):
        place_in = groups[stage][1]
        trace_out[stage] = value
        trace_in[stage, place_in] = value
        copies = []
        for k, partner in enumerate(groups[stage][2]):
            copies.append(
                pltpu.make_async_remote_copy(
                    src_ref=trace_out.at[stage],
                    dst_ref=trace_in.at[stage, place_in],
                    send_sem=trace_send.at[stage, k],
                    recv_sem=trace_recv.at[stage, k],
                    device_id=partner,
                    device_id_type=MESH,
                )
            )
            copies[-1].start()
        return copies

    def take(stage, copies):
        for copy in copies:
            copy.wait_recv()
        total = trace_in[stage, 0]
        for k in range(1, groups[stage][0]):
            total = total + trace_in[stage, k]
        return total

    first_copies = give(0, jnp.full((1, 128), trace, F32))
    square = 1.5 * once - 0.5 * apply(twice)
    once = apply(square)
    cube = 1.5 * once - 0.5 * apply(apply(once))
    last = 1.5 * first - 0.5 * cube
    for i in range(blocks):
        part = last[:, i * edge : (i + 1) * edge].T
        results[i] = 0.5 * (jnp.where(diagonal, 1.0, 0.0) - part) if i == 0 else -0.5 * part
    results[blocks] = jnp.zeros((edge, edge), F32)
    returns = []
    for r in (0, 2, 1):
        for k in range(BACK):
            if r == 1:
                back[1, k] = results[chosen[r][k]]
            else:
                going[r // 2, k] = results[chosen[r][k]]
        if r != 1:
            returns.append(
                pltpu.make_async_remote_copy(
                    src_ref=going.at[r // 2],
                    dst_ref=back.at[2 - r],
                    send_sem=back_send.at[r // 2],
                    recv_sem=back_recv.at[r // 2],
                    device_id=(near[r], column),
                    device_id_type=MESH,
                )
            )
            returns[-1].start()
    total = take(0, first_copies)
    pl.semaphore_wait(ready.at[final], 2)
    last_copies = give(1, total)
    for copy in returns:
        copy.wait()
    weights = [
        [jnp.where(stored[r][k] == t, 1.0, 0.0).astype(F32) for r in range(3) for k in range(BACK)]
        for t in range(tiles_per)
    ]
    for at in range(0, edge, 8):
        pieces = [back[r, k, pl.ds(at, 8)] for r in range(3) for k in range(BACK)]
        for t in range(tiles_per):
            total = weights[t][0] * pieces[0]
            for weight, piece in zip(weights[t][1:], pieces[1:]):
                total = total + weight * piece
            out_ref[t, pl.ds(at, 8)] = total
    for copy in first_copies + last_copies:
        copy.wait_send()
    elec_ref[...] = jnp.broadcast_to(2.0 * take(1, last_copies), elec_ref.shape)


def on_device(ks_tiles, chem_shift, spectral_scale, sub_tiles, result_dest):
    owners = lax.axis_size("owner")
    columns = lax.axis_size("col")
    tiles_per, edge = ks_tiles.shape[0], ks_tiles.shape[1]
    blocks = sub_tiles.shape[1]
    order = blocks * edge
    widest = max(2 * columns, owners // 2)
    vmem, smem, hbm = pltpu.VMEM, pltpu.SMEM, pl.ANY
    dma = pltpu.SemaphoreType.DMA
    density, electrons = pl.pallas_call(
        functools.partial(kernel, owners, columns, blocks),
        out_shape=(
            jax.ShapeDtypeStruct((tiles_per, edge, edge), F32),
            jax.ShapeDtypeStruct((8, 128), F32),
        ),
        in_specs=[pl.BlockSpec(memory_space=vmem)] * 2 + [pl.BlockSpec(memory_space=hbm)] * 3,
        out_specs=[pl.BlockSpec(memory_space=vmem)] * 2,
        scratch_shapes=[
            vmem((tiles_per, edge, edge), BF16),
            vmem((blocks, blocks, owners * columns), jnp.int32),
            vmem((blocks, owners * columns), jnp.int32),
            vmem((3 * columns * ROOM, edge, edge), BF16),
            vmem((tiles_per, edge, edge), BF16),
            vmem((3 * columns * ROOM + 1, edge, edge), BF16),
            smem((blocks * blocks,), jnp.int32),
            vmem((order, order), BF16),
            vmem((order, order), BF16),
            vmem((blocks + 1, edge, edge), F32),
            vmem((2, BACK, edge, edge), F32),
            vmem((3, BACK, edge, edge), F32),
            vmem((2, 1, 128), F32),
            vmem((2, widest, 1, 128), F32),
            dma((3,)),
            dma((2,)),
            dma((3 * columns,)),
            dma((3 * columns,)),
            dma((2,)),
            dma((2,)),
            dma((2, widest)),
            dma((2, widest)),
            pltpu.SemaphoreType.REGULAR((2 + log2(owners),)),
        ],
        compiler_params=pltpu.CompilerParams(
            collective_id=0, has_side_effects=True, vmem_limit_bytes=48 * 2**20
        ),
        name="submatrix_density",
    )(
        chem_shift.reshape(1, 1),
        spectral_scale.reshape(1, 1),
        *(
            pltpu.with_memory_space_constraint(a, pltpu.HBM)
            for a in (
                ks_tiles,
                jnp.transpose(sub_tiles, (1, 2, 0)),
                result_dest.T,
            )
        )
    )
    return density, electrons[0, :1]


def solution(mesh):
    return jax.shard_map(
        on_device,
        mesh=mesh,
        in_specs=(P(("owner", "col"), None, None), P(), P(), P(), P()),
        out_specs=(P(("owner", "col"), None, None), P()),
        check_vma=False,
    )
```

```python
import functools
import itertools
import jax
import jax.numpy as jnp
from jax import lax
from jax.experimental import pallas as pl
from jax.experimental.pallas import tpu as pltpu
from jax.sharding import PartitionSpec as P

F32 = jnp.float32
BF16 = jnp.bfloat16
MESH = pl.DeviceIdType.MESH
ROOM = 2
BACK = 3
FAR = 1 << 20


def log2(n):
    assert n & (n - 1) == 0
    return n.bit_length() - 1


def dot(a, b):
    return jnp.dot(a, b, preferred_element_type=F32)


def kernel(
    owners, columns, blocks, chem_ref, scale_ref, tiles_hbm, sub_hbm, dest_hbm,
    out_ref, elec_ref, tiles_ref, lists, dests, packet, passing, arrived, place, high, low,
    results, going, back, trace_out, trace_in, fetch_sem, pass_sem, send_sem, recv_sem, back_send, back_recv,
    trace_send, trace_recv, ready,
):
    tiles_per, edge = tiles_ref.shape[0], tiles_ref.shape[1]
    devices = owners * columns
    owner = lax.axis_index("owner")
    column = lax.axis_index("col")
    myself = owner * columns + column
    tile_bits, column_bits = log2(tiles_per), log2(columns)
    near = [lax.rem(owner + owners + r - 1, owners) for r in range(3)]
    half = columns // 2
    core = owner & 1
    turn = 1 - 2 * core
    at = [lax.rem(column + turn * k + columns, columns) for k in range(columns)]
    before = at[columns - 1]

    fetches = [
        pltpu.make_async_copy(there, here, fetch_sem.at[n])
        for n, (there, here) in enumerate(
            (
                (sub_hbm, lists),
                (tiles_hbm, tiles_ref),
                (dest_hbm, dests),
            )
        )
    ]
    for fetch in fetches:
        fetch.start()
    beside = [(owner, at[1]), (owner, before), (near[0], column), (near[2], column)]
    barrier = pltpu.get_barrier_semaphore()

    def tell(sem, partners):
        for partner in partners:
            pl.semaphore_signal(sem, inc=1, device_id=partner, device_id_type=MESH)

    tell(barrier, beside)
    pl.semaphore_wait(barrier, len(beside))

    step = pltpu.make_async_remote_copy(
        src_ref=tiles_hbm,
        dst_ref=passing,
        send_sem=pass_sem.at[0],
        recv_sem=pass_sem.at[1],
        device_id=(owner, at[1]),
        device_id_type=MESH,
    )
    step.start()
    tell(ready.at[0], beside)
    for fetch in fetches:
        fetch.wait()

    shape = (blocks, devices)
    lane = lax.broadcasted_iota(jnp.int32, shape, 1)
    row = lax.broadcasted_iota(jnp.int32, shape, 0)

    def asked_of(source):
        least, most = jnp.full(shape, FAR, jnp.int32), jnp.full(shape, -1, jnp.int32)
        for i in range(blocks):
            asked = lists[i]
            mine = lax.shift_right_arithmetic(asked, tile_bits) == source
            code = (row + i * blocks) * tiles_per + (asked & (tiles_per - 1))
            least = jnp.minimum(least, jnp.where(mine, code, FAR))
            most = jnp.maximum(most, jnp.where(mine, code, -1))
        least = jnp.min(least, axis=0, keepdims=True) & (tiles_per - 1)
        most = jnp.max(most, axis=0, keepdims=True) & (tiles_per - 1)
        return least * tiles_per + most

    sends = []

    def pack(asked, tiles, r, to, ref, slot):
        both = jnp.sum(jnp.where(lane[:1] == near[r] * columns + to, asked, 0))
        ref[slot] = tiles[lax.shift_right_arithmetic(both, tile_bits)]
        ref[slot + 1] = tiles[both & (tiles_per - 1)]

    def send(asked, tiles, r, k, source, to):
        slot = (r * columns + k) * ROOM
        pack(asked, tiles, r, to, packet, slot)
        sends.append(
            pltpu.make_async_remote_copy(
                src_ref=packet.at[pl.ds(slot, ROOM)],
                dst_ref=arrived.at[pl.ds(((2 - r) * columns + source) * ROOM, ROOM)],
                send_sem=send_sem.at[r * columns + k],
                recv_sem=recv_sem.at[r * columns + k],
                device_id=(near[r], to),
                device_id_type=MESH,
            )
        )
        sends[-1].start()

    asked = asked_of(myself)
    pl.semaphore_wait(ready.at[0], len(beside))
    over = [(owner, at[2]), (owner, at[columns - 2])]
    tell(ready.at[1], over)
    for k in (columns - 1, 0):
        for r in range(3):
            if (r, k) != (1, 0):
                send(asked, tiles_ref, r, k, column, at[k])
    pl.semaphore_wait(ready.at[1], len(over))
    for k in range(columns - 2, half, -1):
        for r in range(3):
            send(asked, tiles_ref, r, k, column, at[k])
    pack(asked, tiles_ref, 1, column, arrived, (columns + column) * ROOM)
    asked = asked_of(owner * columns + before)

    nothing = 3 * columns * ROOM
    arrived[nothing] = jnp.zeros((edge, edge), BF16)
    across_i = lax.broadcasted_iota(jnp.int32, (blocks, blocks), 1)
    spot = across_i * blocks + lax.broadcasted_iota(jnp.int32, (blocks, blocks), 0)
    own = jnp.zeros((blocks, blocks), jnp.int32)
    for i in range(blocks):
        held = jnp.sum(jnp.where(lane == myself, lists[i], 0), axis=1, keepdims=True)
        own = own + jnp.where(across_i == i, held, 0)
    source = lax.shift_right_arithmetic(own, tile_bits)
    offset = lax.shift_right_arithmetic(source, column_bits) - owner + (owners + 1)
    offset = jnp.where(offset >= owners, offset - owners, offset)
    offset = jnp.where(offset >= owners, offset - owners, offset)
    base = (offset * columns + (source & (columns - 1))) * ROOM
    for p in range(blocks * blocks):
        here = spot == p
        entry = jnp.sum(jnp.where(here, own, 0))
        start = jnp.sum(jnp.where(here, base, 0))
        same = source == lax.shift_right_arithmetic(entry, tile_bits)
        rank = (jnp.min(jnp.where(same, spot, FAR)) < p).astype(jnp.int32)
        place[p] = jnp.where(entry >= 0, jnp.clip(start + rank, 0, nothing), nothing)

    step.wait()
    for k in range(half, 0, -1):
        for r in range(3):
            if (r, k) != (1, 1):
                send(asked, passing, r, k, before, at[k - 1])
    pack(asked, passing, 1, column, arrived, (columns + before) * ROOM)

    reach, stage = 1, 2
    while 2 * reach <= max(2, owners // 2):
        far = [
            (lax.rem(owner + reach, owners), column),
            (lax.rem(owner + owners - reach, owners), column),
        ]
        tell(ready.at[stage], far)
        pl.semaphore_wait(ready.at[stage], 2)
        reach, stage = 2 * reach, stage + 1

    targets = [
        [
            jnp.sum(jnp.where((lane == near[r] * columns + column) & (row == i), dests[...], 0))
            for i in range(blocks)
        ]
        for r in range(3)
    ]
    chosen = [[jnp.int32(blocks) for _ in range(BACK)] for _ in range(3)]
    stored = [[jnp.int32(-1) for _ in range(BACK)] for _ in range(3)]
    for r in range(3):
        taken = jnp.int32(0)
        sent = jnp.int32(0)
        for i in range(blocks):
            target = targets[r][i]
            home = lax.shift_right_arithmetic(target, tile_bits + column_bits)
            mine = (target >= 0) & (home == owner)
            for k in range(BACK):
                stored[r][k] = jnp.where(mine & (taken == k), target & (tiles_per - 1), stored[r][k])
            taken = taken + mine.astype(jnp.int32)
            target = targets[1][i]
            home = lax.shift_right_arithmetic(target, tile_bits + column_bits)
            theirs = (target >= 0) & (home == near[r])
            for k in range(BACK):
                chosen[r][k] = jnp.where(theirs & (sent == k), i, chosen[r][k])
            sent = sent + theirs.astype(jnp.int32)

    for copy in sends:
        copy.wait()

    chem = chem_ref[...]
    inverse = 1.0 / scale_ref[...]
    order = blocks * edge
    wide = 2 * edge
    diagonal = lax.broadcasted_iota(jnp.int32, (edge, edge), 0) == lax.broadcasted_iota(
        jnp.int32, (edge, edge), 1
    )
    parts = []
    for i, j in sorted(itertools.product(range(blocks), repeat=2), key=lambda p: (p[0] > 0, p[1])):
        part = arrived[place[i * blocks + j]].astype(F32)
        part = part + arrived[place[j * blocks + i]].T.astype(F32)
        part = part * (0.5 * inverse)
        if i == j:
            part = part - jnp.where(diagonal, chem * inverse, 0.0)
        rows, cols = pl.ds(i * edge, edge), pl.ds(j * edge, edge)
        upper = part.astype(BF16)
        high[rows, cols] = upper
        low[rows, cols] = (part - upper.astype(F32)).astype(BF16)
        if i == 0:
            parts.append(part)
    start = jnp.concatenate(parts, axis=1)

    def apply(u):
        upper = u.astype(BF16)
        lower = (u - upper.astype(F32)).astype(BF16)
        both = jnp.concatenate([upper, lower], axis=0)
        parts = []
        for at in range(0, order, wide):
            cut = pl.ds(at, wide)
            w = dot(both, high[:, cut])
            parts.append(w[:edge] + w[edge:] + dot(upper, low[:, cut]))
        return jnp.concatenate(parts, axis=1)

    first = 1.5 * start - 0.5 * apply(apply(start))
    once = apply(first)
    twice = apply(once)
    cubed = 1.5 * jnp.sum(first * once) - 0.5 * jnp.sum(once * twice)
    trace = 1.5 * jnp.sum(jnp.where(diagonal, first[:, :edge], 0.0)) - 0.5 * cubed
    trace = 0.5 * (edge - trace)

    inner = min(8, owners)
    width, depth = inner // 2, owners // inner
    here_x, here_z = lax.div(lax.rem(owner, inner), 2), lax.div(owner, inner)

    def steps(*sizes):
        every = list(itertools.product(*(range(size) for size in sizes)))[1:]
        return sorted(every, key=lambda p: -sum(min(n, size - n) for n, size in zip(p, sizes)))

    groups = (
        (columns, column, [(owner, lax.rem(column + dy, columns)) for (dy,) in steps(columns)]),
        (
            inner,
            lax.rem(owner, inner),
            [
                (here_z * inner + lax.rem(here_x + dx, width) * 2 + lax.rem(core + dc, 2), column)
                for dx, dc in steps(width, 2)
            ],
        ),
        (
            depth,
            here_z,
            [(lax.rem(owner + dz * inner, owners), column) for (dz,) in steps(depth)],
        ),
    )

    def give(stage, value):
        place_in = groups[stage][1]
        trace_out[stage] = value
        trace_in[stage, place_in] = value
        copies = []
        for k, partner in enumerate(groups[stage][2]):
            copies.append(
                pltpu.make_async_remote_copy(
                    src_ref=trace_out.at[stage],
                    dst_ref=trace_in.at[stage, place_in],
                    send_sem=trace_send.at[stage, k],
                    recv_sem=trace_recv.at[stage, k],
                    device_id=partner,
                    device_id_type=MESH,
                )
            )
            copies[-1].start()
        return copies

    def take(stage, copies):
        for copy in copies:
            copy.wait_recv()
        total = trace_in[stage, 0]
        for k in range(1, groups[stage][0]):
            total = total + trace_in[stage, k]
        return total

    first_copies = give(0, jnp.full((1, 128), trace, F32))
    square = 1.5 * once - 0.5 * apply(twice)
    once = apply(square)
    cube = 1.5 * once - 0.5 * apply(apply(once))
    last = 1.5 * first - 0.5 * cube
    for i in range(blocks):
        part = last[:, i * edge : (i + 1) * edge].T
        results[i] = 0.5 * (jnp.where(diagonal, 1.0, 0.0) - part) if i == 0 else -0.5 * part
    results[blocks] = jnp.zeros((edge, edge), F32)
    returns = []
    for r in (0, 2, 1):
        for k in range(BACK):
            if r == 1:
                back[1, k] = results[chosen[r][k]]
            else:
                going[r // 2, k] = results[chosen[r][k]]
        if r != 1:
            returns.append(
                pltpu.make_async_remote_copy(
                    src_ref=going.at[r // 2],
                    dst_ref=back.at[2 - r],
                    send_sem=back_send.at[r // 2],
                    recv_sem=back_recv.at[r // 2],
                    device_id=(near[r], column),
                    device_id_type=MESH,
                )
            )
            returns[-1].start()
    next_copies = give(1, take(0, first_copies))
    for copy in returns:
        copy.wait()
    last_copies = give(2, take(1, next_copies))
    weights = [
        [jnp.where(stored[r][k] == t, 1.0, 0.0).astype(F32) for r in range(3) for k in range(BACK)]
        for t in range(tiles_per)
    ]
    for at in range(0, edge, 8):
        pieces = [back[r, k, pl.ds(at, 8)] for r in range(3) for k in range(BACK)]
        for t in range(tiles_per):
            total = weights[t][0] * pieces[0]
            for weight, piece in zip(weights[t][1:], pieces[1:]):
                total = total + weight * piece
            out_ref[t, pl.ds(at, 8)] = total
    for copy in first_copies + next_copies + last_copies:
        copy.wait_send()
    elec_ref[...] = jnp.broadcast_to(2.0 * take(2, last_copies), elec_ref.shape)


def on_device(ks_tiles, chem_shift, spectral_scale, sub_tiles, result_dest):
    owners = lax.axis_size("owner")
    columns = lax.axis_size("col")
    tiles_per, edge = ks_tiles.shape[0], ks_tiles.shape[1]
    blocks = sub_tiles.shape[1]
    order = blocks * edge
    widest = max(columns, min(8, owners), owners // 8)
    vmem, smem, hbm = pltpu.VMEM, pltpu.SMEM, pl.ANY
    dma = pltpu.SemaphoreType.DMA
    density, electrons = pl.pallas_call(
        functools.partial(kernel, owners, columns, blocks),
        out_shape=(
            jax.ShapeDtypeStruct((tiles_per, edge, edge), F32),
            jax.ShapeDtypeStruct((8, 128), F32),
        ),
        in_specs=[pl.BlockSpec(memory_space=vmem)] * 2 + [pl.BlockSpec(memory_space=hbm)] * 3,
        out_specs=[pl.BlockSpec(memory_space=vmem)] * 2,
        scratch_shapes=[
            vmem((tiles_per, edge, edge), BF16),
            vmem((blocks, blocks, owners * columns), jnp.int32),
            vmem((blocks, owners * columns), jnp.int32),
            vmem((3 * columns * ROOM, edge, edge), BF16),
            vmem((tiles_per, edge, edge), BF16),
            vmem((3 * columns * ROOM + 1, edge, edge), BF16),
            smem((blocks * blocks,), jnp.int32),
            vmem((order, order), BF16),
            vmem((order, order), BF16),
            vmem((blocks + 1, edge, edge), F32),
            vmem((2, BACK, edge, edge), F32),
            vmem((3, BACK, edge, edge), F32),
            vmem((3, 1, 128), F32),
            vmem((3, widest, 1, 128), F32),
            dma((3,)),
            dma((2,)),
            dma((3 * columns,)),
            dma((3 * columns,)),
            dma((2,)),
            dma((2,)),
            dma((3, widest)),
            dma((3, widest)),
            pltpu.SemaphoreType.REGULAR((2 + log2(owners),)),
        ],
        compiler_params=pltpu.CompilerParams(
            collective_id=0, has_side_effects=True, vmem_limit_bytes=48 * 2**20
        ),
        name="submatrix_density",
    )(
        chem_shift.reshape(1, 1),
        spectral_scale.reshape(1, 1),
        *(
            pltpu.with_memory_space_constraint(a, pltpu.HBM)
            for a in (
                ks_tiles,
                jnp.transpose(sub_tiles, (1, 2, 0)),
                result_dest.T,
            )
        )
    )
    return density, electrons[0, :1]


def solution(mesh):
    return jax.shard_map(
        on_device,
        mesh=mesh,
        in_specs=(P(("owner", "col"), None, None), P(), P(), P(), P()),
        out_specs=(P(("owner", "col"), None, None), P()),
        check_vma=False,
    )
```
